32 devices in a mesh: groups: 2 (over x), expert: 16 (over z, y, core).
Axes of the slice: x: 2, y: 2, z: 4, core: 2. Of those that a mesh axis runs over, the one named last changes fastest.
Arguments:
- residual: bfloat16 [512, 2880], P(('groups', 'expert')), parts along dimension 0, may hold values from -6 to 6
- norm_gain: float32 [2880], replicated, may hold values from 0.1 to 1.9
- expert_ids: int32 [512, 4], P(('groups', 'expert')), parts along dimension 0, may hold values from 0 to 7, all different within a row; in each aligned block of 16 rows (0 to 15, 16 to 31, ...) at most 16 rows name the same one
- expert_weights: float32 [512, 4], P(('groups', 'expert')), parts along dimension 0, may hold values from 0.2 to 1
- gate_proj: bfloat16 [16, 2880, 720], P('expert'), may hold values from -0.109375 to 0.109375
- up_proj: bfloat16 [16, 2880, 720], P('expert'), may hold values from -0.109375 to 0.109375
- down_proj: bfloat16 [16, 720, 2880], P('expert'), may hold values from -0.15625 to 0.15625
Outputs:
- mixed: bfloat16 [512, 2880], P(('groups', 'expert')), parts along dimension 0
The draws below stay inside these ranges and needn't reach their ends.
There are 2 independent parts, one for each index of `groups`. The reference program is written for one: setup_inputs(seed, part) draws one part's arguments, and reference() takes and returns one part's arrays. A program takes and returns all parts, laid end to end along the dimension named above; an argument that names none is the same for every part. Nothing has to cross between parts.
Inputs may be any that keep to these rules, and one draw needn't show every extreme that they name: `expert_ids`: in each aligned block of 16 rows (the rows of one device) no expert is named by more than 16 entries.
All inputs are finite; a program needn't handle non-finite values.
Results may differ from the reference program's by a relative error of at most 0.0063.
Values may be sent and summed in bfloat16 or wider, within the bound.
No kernel may reach another device: no remote copies, remote signals or barrier semaphores. Data moves between devices by JAX's collectives and lax.ppermute only.
A program may use at most 64 MiB of HBM per device.

```python
import math
import jax
import jax.numpy as jnp
import numpy as np
from jax import lax

D = 2880
FF = 1440
HALF = 720
TOP = 4
EXPERTS = 8
REQ_DEV = 16
CAP = 16
TOKENS = 256
N_EXPERT = 16


def block_levels(key, dims, pieces, low, largest):
    def one(position, blocks):
        steps = jax.random.uniform(jax.random.fold_in(jax.random.fold_in(key, 6), position), (blocks,), jnp.float32, low / len(pieces), largest / len(pieces))
        return jnp.repeat(jnp.exp(steps), dims[position] // blocks).reshape((-1,) + (1,) * (len(dims) - position - 1))

    factor_of = one(*pieces[0])
    for cut in pieces[1:]:
        factor_of = factor_of * one(*cut)
    return factor_of


def deal_out(own_key, own, number, rows, count, top, bound, lean):
    sequence = jax.random.permutation(own_key, count)
    packed, usual = portions_of(count, rows * top, bound, lean, True), portions_of(count, rows * top, bound, lean, False)
    places = jnp.arange(count)

    def named(sizes, rotation):
        used = int((sizes > 0).sum())
        fixed = max(1, used // 4)
        shifted = fixed + (places - fixed + rotation * (used - fixed)) % max(1, count - fixed)
        return jnp.zeros((count,), jnp.int32).at[sequence[jnp.where(places < fixed, places, shifted)]].set(jnp.asarray(sizes, jnp.int32))

    sizes = jnp.where(number % 4 == 0, named(packed, number // 4), named(usual, number - number // 4 - 1))
    mixed = jax.random.permutation(jax.random.fold_in(own, 3), count)
    donor, taker = mixed[0:count // 2 * 2:2], mixed[1:count // 2 * 2:2]
    room = jnp.minimum(sizes[donor] - 1, bound - sizes[taker]) // 2
    room = jnp.where((donor == sequence[0]) | (taker == sequence[0]) | (sizes[taker] == 0), 0, jnp.maximum(room, 0))
    shifted = jax.random.randint(jax.random.fold_in(own, 4), (count // 2,), 0, 1 << 20) % (room + 1)
    sizes = sizes.at[donor].add(-shifted).at[taker].add(shifted)
    items = jnp.searchsorted(jnp.cumsum(sizes), jnp.arange(rows * top), side="right").astype(jnp.int32)
    grid = items.reshape(top, rows).T
    grid = grid[jax.random.permutation(jax.random.fold_in(own, 1), rows)]
    rotation = jax.random.randint(jax.random.fold_in(own, 2), (rows, 1), 0, top)
    return jnp.take_along_axis(grid, (jnp.arange(top)[None, :] + rotation) % top, axis=1)


def portions_of(amount, total, most, lean, full):
    loads = [(1 << 20) // math.isqrt(grade ** lean) + 1 for grade in range(1, amount + 1)]
    largest = most if full else min(most, max(-(-total // amount), total * loads[0] // sum(loads)))
    least = 1 if total - largest >= amount - 1 else 0
    counts, rest = [largest] + [least] * (amount - 1), total - largest - least * (amount - 1)
    while rest > 0:
        candidates = [i for i in range(1, amount) if counts[i] < largest] or [i for i in range(1, amount) if counts[i] < most]
        pool, left = sum([loads[i] for i in candidates]), rest
        for i in candidates:
            addition = min(most - counts[i], max(1, left * loads[i] // pool), rest)
            counts[i] = counts[i] + addition
            rest = rest - addition
    return np.array(counts)


def normal_values(stream_key, shape, scale, bound, shards=(), dtype=jnp.bfloat16):
    factor_of = block_levels(stream_key, shape, shards, -0.22, 0.18) if shards else 1.0
    array = jax.random.normal(stream_key, shape, jnp.float32) * scale * factor_of
    return jnp.minimum(jnp.maximum(array, -bound), bound).astype(dtype)


def setup_inputs(seed: int = 0, part: int = 0) -> dict:
    streams_of = jax.random.split(jax.random.key(seed), 8)
    own_keys = jax.random.split(jax.random.fold_in(streams_of[7], part), 8)
    residual = normal_values(own_keys[0], (TOKENS, D), 1.0, 6.0, ((0, 16),))
    norm_gain = jnp.clip(1.0 + 0.18 * jax.random.normal(streams_of[1], (D,), jnp.float32), 0.1, 1.9)
    expert_ids_keys = jax.random.split(jax.random.fold_in(own_keys[2], 1), TOKENS // REQ_DEV)
    expert_ids_turns = jax.random.permutation(jax.random.fold_in(own_keys[2], 3), TOKENS // REQ_DEV)
    expert_ids = jax.vmap(lambda own, number: deal_out(jax.random.fold_in(own_keys[2], 2), own, number, REQ_DEV, EXPERTS, TOP, CAP, 2))(expert_ids_keys, expert_ids_turns).reshape((TOKENS, TOP))
    expert_weights = jnp.clip(0.2 + 0.8 * jax.random.uniform(own_keys[3], (TOKENS, TOP), jnp.float32) ** block_levels(own_keys[3], (TOKENS, TOP), ((0, 16),), -0.2, 0.2), 0.2, 1.0)
    gate_proj = normal_values(streams_of[4], (2 * EXPERTS, D, HALF), D ** -0.5, 0.109375, ((0, 16),))
    up_proj = normal_values(streams_of[5], (2 * EXPERTS, D, HALF), D ** -0.5, 0.109375, ((0, 16),))
    down_proj = normal_values(streams_of[6], (2 * EXPERTS, HALF, D), FF ** -0.5, 0.15625, ((0, 16),))
    return {"residual": residual, "norm_gain": norm_gain, "expert_ids": expert_ids, "expert_weights": expert_weights, "gate_proj": gate_proj, "up_proj": up_proj, "down_proj": down_proj}


def expert_half(flat, gate_w, up_w, down_w):
    gate = jnp.dot(flat, gate_w, preferred_element_type=jnp.float32)
    upper = jnp.dot(flat, up_w, preferred_element_type=jnp.float32)
    act = (gate * jax.nn.sigmoid(1.702 * gate) * (upper + 1.0)).astype(jnp.bfloat16)
    return jnp.dot(act, down_w, preferred_element_type=jnp.float32).astype(jnp.bfloat16)

def reference(residual, norm_gain, expert_ids, expert_weights, gate_proj, up_proj, down_proj):
    devices = N_EXPERT
    experts = devices // 2
    width = REQ_DEV * TOP
    x = residual.astype(jnp.float32)
    scale = lax.rsqrt(lax.optimization_barrier(jnp.mean(x * x, axis=-1, keepdims=True)) + 1e-05)
    normed = (x * scale * norm_gain.astype(jnp.float32)).astype(jnp.bfloat16)
    flat = expert_ids.reshape(devices, width).astype(jnp.int32)
    onehot = (flat[:, :, None] == jnp.arange(experts).astype(jnp.int32)[None, None, :]).astype(jnp.int32)
    slot = (lax.optimization_barrier(jnp.sum(onehot * jnp.cumsum(onehot, axis=1), axis=-1)) - 1).astype(jnp.int32)
    source = jnp.broadcast_to(jnp.arange(devices).astype(jnp.int32)[:, None], (devices, width))
    token = (jnp.arange(width).astype(jnp.int32) // TOP)[None, :] + source * REQ_DEV
    buffer = jnp.zeros((experts, devices, CAP, D), jnp.bfloat16).at[flat, source, slot].set(normed[token])

    def run(items):
        block, gate_w, up_w, down_w = items
        first = expert_half(block, gate_w[0], up_w[0], down_w[0])
        second = expert_half(block, gate_w[1], up_w[1], down_w[1])
        return (first.astype(jnp.float32) + second.astype(jnp.float32)).astype(jnp.bfloat16)
    outs = lax.map(run, (buffer.reshape(experts, devices * CAP, D), gate_proj.reshape(experts, 2, D, HALF), up_proj.reshape(experts, 2, D, HALF), down_proj.reshape(experts, 2, HALF, D)))
    outs = outs.reshape(experts, devices, CAP, D)
    picked = outs[flat, source, slot].reshape(devices, REQ_DEV, TOP, D).astype(jnp.float32)
    weights = expert_weights.reshape(devices, REQ_DEV, TOP, 1)
    mixed = x.reshape(devices, REQ_DEV, D) + lax.optimization_barrier(jnp.sum(weights * picked, axis=2))
    return mixed.reshape(TOKENS, D).astype(jnp.bfloat16)
```

```python
import jax
import jax.numpy as jnp
from jax import lax
from jax.sharding import PartitionSpec as P


def partner(value, axis, bit):
    mask = 2**bit
    pairs = [(source, source ^ mask) for source in range(lax.axis_size(axis))]
    return lax.ppermute(value, axis, pairs)


def expert_half(flat, gate_w, up_w, down_w):
    gate = jnp.dot(flat, gate_w, preferred_element_type=jnp.float32)
    upper = jnp.dot(flat, up_w, preferred_element_type=jnp.float32)
    act = (gate * jax.nn.sigmoid(1.702 * gate) * (upper + 1.0)).astype(jnp.bfloat16)
    return jnp.dot(act, down_w, preferred_element_type=jnp.float32).astype(jnp.bfloat16)


def normalised(rows, norm_gain):
    x = rows.astype(jnp.float32)
    scale = lax.rsqrt(jnp.mean(x * x, axis=-1, keepdims=True) + 1e-05)
    return (x * scale * norm_gain).astype(jnp.bfloat16)


def pair_sum(mine, theirs):
    return (mine.astype(jnp.float32) + theirs.astype(jnp.float32)).astype(jnp.bfloat16)


def slots(residual, norm_gain, expert_ids, expert_weights, gate_proj, up_proj, down_proj):
    rows, model = residual.shape
    chosen = expert_ids.shape[1]
    devices = lax.axis_size("expert")
    experts = devices // 2
    capacity = 2 * rows * chosen // experts
    half_cap = capacity // 2
    gate_w, up_w, down_w = (gate_proj[0], up_proj[0], down_proj[0])
    normed = normalised(residual, norm_gain)
    flat_ids = expert_ids.reshape(rows * chosen)
    onehot = (
        flat_ids[:, None] == lax.broadcasted_iota(jnp.int32, (rows * chosen, experts), 1)
    ).astype(jnp.int32)
    slot = jnp.sum(onehot * jnp.cumsum(onehot, axis=0), axis=1) - 1
    position = flat_ids * capacity + slot
    pick = (
        position[:, None] == lax.broadcasted_iota(jnp.int32, (rows * chosen, experts * capacity), 1)
    ).astype(jnp.float32)
    place_rows = jnp.sum(pick.reshape(rows, chosen, experts * capacity), axis=1)
    send = lax.dot_general(
        place_rows.astype(jnp.bfloat16),
        normed,
        (((0,), (0,)), ((), ())),
        preferred_element_type=jnp.float32,
    )
    outgoing = send.astype(jnp.bfloat16).reshape(devices, half_cap, model)
    arrived = lax.all_to_all(outgoing, "expert", split_axis=0, concat_axis=0, tiled=True)
    other = partner(arrived, "expert", 0)
    both = jnp.stack((arrived, other)).reshape(2 * devices * half_cap, model)
    both = expert_half(both, gate_w, up_w, down_w).reshape(2, devices, half_cap, model)
    returned = partner(both[1], "expert", 0)
    finished = pair_sum(both[0], returned)
    back = lax.all_to_all(finished, "expert", split_axis=0, concat_axis=0, tiled=True)
    weighted = jnp.sum(
        (pick * expert_weights.reshape(rows * chosen)[:, None]).reshape(
            rows, chosen, experts * capacity
        ),
        axis=1,
    )
    combined = jnp.dot(
        weighted,
        back.reshape(experts * capacity, model).astype(jnp.float32),
        precision=lax.Precision.HIGHEST,
    )
    return (residual.astype(jnp.float32) + combined).astype(jnp.bfloat16)


def ring_order(chips):
    return list(range(0, chips, 2)) + list(range(1, chips, 2))[::-1]


def ring(residual, norm_gain, expert_ids, expert_weights, gate_proj, up_proj, down_proj):
    rows, model = residual.shape
    devices = lax.axis_size("expert")
    chips = devices // 2
    far = chips // 2
    order = ring_order(chips)
    gate_w, up_w, down_w = (gate_proj[0], up_proj[0], down_proj[0])
    me = lax.axis_index("expert")
    core = me % 2

    def at(position, of_core):
        return 2 * order[position % chips] + of_core

    def ringwise(value, hops):
        pairs = [(at(i, 0), at(i + hops, 0)) for i in range(chips)]
        pairs += [(at(i, 1), at(i - hops, 1)) for i in range(chips)]
        return lax.ppermute(value, "expert", pairs)

    def swap(value):
        return partner(value, "expert", 0)

    def expert_at(hops):
        table = [0] * devices
        for i in range(chips):
            table[at(i, 0)] = order[(i + hops) % chips]
            table[at(i, 1)] = order[(i - hops) % chips]
        return jnp.take(jnp.array(table, jnp.int32), me)

    def weight_of(ids, weights, hops):
        return jnp.sum(jnp.where(ids == expert_at(hops), weights, 0.0), axis=1, keepdims=True)

    def run(block):
        return expert_half(normalised(block, norm_gain), gate_w, up_w, down_w)

    x = residual
    away = ringwise(x, far)
    chip_rows = jnp.concatenate((x, swap(x)))
    ids = jnp.concatenate((expert_ids, swap(expert_ids)))
    weights = jnp.concatenate((expert_weights, swap(expert_weights)))
    total = jnp.zeros((2 * rows, model), jnp.float32)
    travelling = chip_rows
    for hops in range(1, far):
        travelling = ringwise(travelling, 1)
        both = jnp.concatenate((travelling, swap(travelling)))
        if hops == 1:
            both = jnp.concatenate((both, chip_rows, away, swap(away)))
        out = run(both)
        block = 2 * rows
        done = pair_sum(out[:block], swap(out[block : 2 * block]))
        total += weight_of(ids, weights, hops) * ringwise(done, -hops).astype(jnp.float32)
        if hops == 1:
            here, there = (out[2 * block : 3 * block], out[3 * block :])
            here = pair_sum(here[:rows], swap(here[rows:]))
            there = pair_sum(there[:rows], swap(there[rows:]))
            own = weight_of(expert_ids, expert_weights, 0) * here.astype(jnp.float32)
            own += weight_of(expert_ids, expert_weights, far) * ringwise(there, far).astype(jnp.float32)
    own += total[:rows] + swap(total[rows:])
    return (x.astype(jnp.float32) + own).astype(jnp.bfloat16)


def body(residual, norm_gain, expert_ids, expert_weights, gate_proj, up_proj, down_proj):
    rows, chosen = expert_ids.shape
    chips = lax.axis_size("expert") // 2
    whole = 2 * rows * chosen // chips >= rows and chips % 4 == 0
    plan = ring if whole else slots
    return plan(residual, norm_gain, expert_ids, expert_weights, gate_proj, up_proj, down_proj)


def solution(mesh):
    in_specs = (
        P(("groups", "expert"), None),
        P(),
        P(("groups", "expert"), None),
        P(("groups", "expert"), None),
        P("expert", None, None),
        P("expert", None, None),
        P("expert", None, None),
    )
    out_specs = P(("groups", "expert"), None)
    return jax.shard_map(body, mesh=mesh, in_specs=in_specs, out_specs=out_specs, check_vma=False)
```

```python
import functools

import jax
import jax.numpy as jnp
from jax import lax
from jax.experimental import pallas as pl
from jax.experimental.pallas import tpu as pltpu
from jax.sharding import PartitionSpec as P


def partner(value, axis, bit):
    mask = 2**bit
    pairs = [(source, source ^ mask) for source in range(lax.axis_size(axis))]
    return lax.ppermute(value, axis, pairs)


def expert_half(flat, gate_w, up_w, down_w):
    gate = jnp.dot(flat, gate_w, preferred_element_type=jnp.float32)
    upper = jnp.dot(flat, up_w, preferred_element_type=jnp.float32)
    act = (gate * jax.nn.sigmoid(1.702 * gate) * (upper + 1.0)).astype(jnp.bfloat16)
    return jnp.dot(act, down_w, preferred_element_type=jnp.float32).astype(jnp.bfloat16)


def normalised(rows, norm_gain):
    x = rows.astype(jnp.float32)
    scale = lax.rsqrt(jnp.mean(x * x, axis=-1, keepdims=True) + 1e-05)
    return (x * scale * norm_gain).astype(jnp.bfloat16)


def pair_sum(mine, theirs):
    return (mine.astype(jnp.float32) + theirs.astype(jnp.float32)).astype(jnp.bfloat16)


def slots(residual, norm_gain, expert_ids, expert_weights, gate_proj, up_proj, down_proj):
    rows, model = residual.shape
    chosen = expert_ids.shape[1]
    devices = lax.axis_size("expert")
    experts = devices // 2
    capacity = 2 * rows * chosen // experts
    half_cap = capacity // 2
    gate_w, up_w, down_w = (gate_proj[0], up_proj[0], down_proj[0])
    normed = normalised(residual, norm_gain)
    flat_ids = expert_ids.reshape(rows * chosen)
    onehot = (
        flat_ids[:, None] == lax.broadcasted_iota(jnp.int32, (rows * chosen, experts), 1)
    ).astype(jnp.int32)
    slot = jnp.sum(onehot * jnp.cumsum(onehot, axis=0), axis=1) - 1
    position = flat_ids * capacity + slot
    pick = (
        position[:, None] == lax.broadcasted_iota(jnp.int32, (rows * chosen, experts * capacity), 1)
    ).astype(jnp.float32)
    place_rows = jnp.sum(pick.reshape(rows, chosen, experts * capacity), axis=1)
    send = lax.dot_general(
        place_rows.astype(jnp.bfloat16),
        normed,
        (((0,), (0,)), ((), ())),
        preferred_element_type=jnp.float32,
    )
    outgoing = send.astype(jnp.bfloat16).reshape(devices, half_cap, model)
    arrived = lax.all_to_all(outgoing, "expert", split_axis=0, concat_axis=0, tiled=True)
    other = partner(arrived, "expert", 0)
    both = jnp.stack((arrived, other)).reshape(2 * devices * half_cap, model)
    both = expert_half(both, gate_w, up_w, down_w).reshape(2, devices, half_cap, model)
    returned = partner(both[1], "expert", 0)
    finished = pair_sum(both[0], returned)
    back = lax.all_to_all(finished, "expert", split_axis=0, concat_axis=0, tiled=True)
    weighted = jnp.sum(
        (pick * expert_weights.reshape(rows * chosen)[:, None]).reshape(
            rows, chosen, experts * capacity
        ),
        axis=1,
    )
    combined = jnp.dot(
        weighted,
        back.reshape(experts * capacity, model).astype(jnp.float32),
        precision=lax.Precision.HIGHEST,
    )
    return (residual.astype(jnp.float32) + combined).astype(jnp.bfloat16)


def expert_kernel(count, *refs):
    blocks, (gain_ref, gate_ref, up_ref, down_ref) = refs[:count], refs[count : count + 4]
    mine_ref, theirs_ref, normed_ref = refs[count + 4 :]
    rows = blocks[0].shape[0]
    for i, block in enumerate(blocks):
        x = block[...].astype(jnp.float32)
        scale = lax.rsqrt(jnp.mean(x * x, axis=-1, keepdims=True) + 1e-05)
        normed_ref[pl.ds(i * rows, rows), :] = (x * scale * gain_ref[...]).astype(jnp.bfloat16)
    normed = normed_ref[...]
    across = (((1,), (1,)), ((), ()))
    gate = lax.dot_general(normed, gate_ref[...], across, preferred_element_type=jnp.float32)
    upper = lax.dot_general(normed, up_ref[...], across, preferred_element_type=jnp.float32)
    act = (gate * jax.nn.sigmoid(1.702 * gate) * (upper + 1.0)).astype(jnp.bfloat16)
    out = jnp.dot(act, down_ref[...], preferred_element_type=jnp.float32).astype(jnp.bfloat16)
    half = rows * (count // 2)
    mine_ref[...] = out[:half]
    theirs_ref[...] = out[half:]


def expert_parts(blocks, gain, gate_w, up_w, down_w):
    count = len(blocks)
    rows, model = blocks[0].shape
    out = jax.ShapeDtypeStruct((rows * count // 2, model), jnp.bfloat16)
    vmem = pl.BlockSpec(memory_space=pltpu.VMEM)
    hidden = gate_w.shape[0]
    return pl.pallas_call(
        functools.partial(expert_kernel, count),
        out_shape=(out, out),
        in_specs=[vmem] * (count + 4),
        out_specs=(vmem, vmem),
        scratch_shapes=[pltpu.VMEM((rows * count, model), jnp.bfloat16)],
        cost_estimate=pl.CostEstimate(
            flops=6 * rows * count * model * hidden,
            bytes_accessed=6 * model * hidden,
            transcendentals=rows * count * hidden,
        ),
        compiler_params=pltpu.CompilerParams(vmem_limit_bytes=24 * 2**20),
    )(*blocks, gain, gate_w, up_w, down_w)


def ring(residual, norm_gain, expert_ids, expert_weights, gate_proj, up_proj, down_proj):
    rows, model = residual.shape
    devices = lax.axis_size("expert")
    chips = devices // 2
    far = chips // 2
    order = list(range(0, chips, 2)) + list(range(1, chips, 2))[::-1]
    held = [
        pltpu.with_memory_space_constraint(w, pltpu.VMEM)
        for w in (gate_proj[0].T, up_proj[0].T, down_proj[0])
    ]
    gain = norm_gain.reshape(1, model)

    def ringwise(value, hops):
        pairs = [
            (2 * order[i] + core, 2 * order[(i + hops) % chips] + core)
            for i in range(chips)
            for core in range(2)
        ]
        return lax.ppermute(value, "expert", pairs)

    def swap(value):
        return partner(value, "expert", 0)

    chip = lax.axis_index("expert") // 2
    place = jnp.where(chip % 2 == 0, chip // 2, chips - 1 - chip // 2)
    on = (place + jnp.arange(chips)) % chips
    expert = jnp.where(on < far, 2 * on, 2 * (chips - 1 - on) + 1)
    weights = jnp.sum(
        jnp.where(expert_ids[:, :, None] == expert[None, None, :], expert_weights[:, :, None], 0.0), axis=1
    )

    x = residual
    arrived = {0: x, far: ringwise(x, far)}
    for way in (1, -1):
        arrived[way] = ringwise(x, way)
    for hops in range(2, far):
        near = hops - 2 if hops > 2 else 1
        for way in (1, -1):
            arrived[way * hops] = ringwise(arrived[way * near], way * (hops - near))
    near = [0, 1, -1, far]
    beyond = [way * hops for hops in range(2, far) for way in (1, -1)]
    finished = {}
    for group in (near, beyond):
        blocks = [arrived[hops] for hops in group]
        mine, theirs = expert_parts(blocks + [swap(block) for block in blocks], gain, *held)
        done = pair_sum(mine, swap(theirs)).reshape(len(group), rows, model)
        for i, hops in enumerate(group):
            finished[hops] = ringwise(done[i], -hops) if hops else done[i]
    combined = jnp.zeros((rows, model), jnp.float32)
    for hops, block in finished.items():
        combined += weights[:, hops % chips][:, None] * block.astype(jnp.float32)
    return (x.astype(jnp.float32) + combined).astype(jnp.bfloat16)


def body(residual, norm_gain, expert_ids, expert_weights, gate_proj, up_proj, down_proj):
    rows, chosen = expert_ids.shape
    chips = lax.axis_size("expert") // 2
    whole = 2 * rows * chosen // chips >= rows and chips % 2 == 0 and chips >= 6
    plan = ring if whole else slots
    return plan(residual, norm_gain, expert_ids, expert_weights, gate_proj, up_proj, down_proj)


def solution(mesh):
    in_specs = (
        P(("groups", "expert"), None),
        P(),
        P(("groups", "expert"), None),
        P(("groups", "expert"), None),
        P("expert", None, None),
        P("expert", None, None),
        P("expert", None, None),
    )
    out_specs = P(("groups", "expert"), None)
    return jax.shard_map(body, mesh=mesh, in_specs=in_specs, out_specs=out_specs, check_vma=False)
```

```python
import functools

import jax
import jax.numpy as jnp
from jax import lax
from jax.experimental import pallas as pl
from jax.experimental.pallas import tpu as pltpu
from jax.sharding import PartitionSpec as P


def partner(value, axis, bit):
    mask = 2**bit
    pairs = [(source, source ^ mask) for source in range(lax.axis_size(axis))]
    return lax.ppermute(value, axis, pairs)


def expert_half(flat, gate_w, up_w, down_w):
    gate = jnp.dot(flat, gate_w, preferred_element_type=jnp.float32)
    upper = jnp.dot(flat, up_w, preferred_element_type=jnp.float32)
    act = (gate * jax.nn.sigmoid(1.702 * gate) * (upper + 1.0)).astype(jnp.bfloat16)
    return jnp.dot(act, down_w, preferred_element_type=jnp.float32).astype(jnp.bfloat16)


def normalised(rows, norm_gain):
    x = rows.astype(jnp.float32)
    scale = lax.rsqrt(jnp.mean(x * x, axis=-1, keepdims=True) + 1e-05)
    return (x * scale * norm_gain).astype(jnp.bfloat16)


def pair_sum(mine, theirs):
    return (mine.astype(jnp.float32) + theirs.astype(jnp.float32)).astype(jnp.bfloat16)


def slots(residual, norm_gain, expert_ids, expert_weights, gate_proj, up_proj, down_proj):
    rows, model = residual.shape
    chosen = expert_ids.shape[1]
    devices = lax.axis_size("expert")
    experts = devices // 2
    capacity = 2 * rows * chosen // experts
    half_cap = capacity // 2
    gate_w, up_w, down_w = (gate_proj[0], up_proj[0], down_proj[0])
    normed = normalised(residual, norm_gain)
    flat_ids = expert_ids.reshape(rows * chosen)
    onehot = (
        flat_ids[:, None] == lax.broadcasted_iota(jnp.int32, (rows * chosen, experts), 1)
    ).astype(jnp.int32)
    slot = jnp.sum(onehot * jnp.cumsum(onehot, axis=0), axis=1) - 1
    position = flat_ids * capacity + slot
    pick = (
        position[:, None] == lax.broadcasted_iota(jnp.int32, (rows * chosen, experts * capacity), 1)
    ).astype(jnp.float32)
    place_rows = jnp.sum(pick.reshape(rows, chosen, experts * capacity), axis=1)
    send = lax.dot_general(
        place_rows.astype(jnp.bfloat16),
        normed,
        (((0,), (0,)), ((), ())),
        preferred_element_type=jnp.float32,
    )
    outgoing = send.astype(jnp.bfloat16).reshape(devices, half_cap, model)
    arrived = lax.all_to_all(outgoing, "expert", split_axis=0, concat_axis=0, tiled=True)
    other = partner(arrived, "expert", 0)
    both = jnp.stack((arrived, other)).reshape(2 * devices * half_cap, model)
    both = expert_half(both, gate_w, up_w, down_w).reshape(2, devices, half_cap, model)
    returned = partner(both[1], "expert", 0)
    finished = pair_sum(both[0], returned)
    back = lax.all_to_all(finished, "expert", split_axis=0, concat_axis=0, tiled=True)
    weighted = jnp.sum(
        (pick * expert_weights.reshape(rows * chosen)[:, None]).reshape(
            rows, chosen, experts * capacity
        ),
        axis=1,
    )
    combined = jnp.dot(
        weighted,
        back.reshape(experts * capacity, model).astype(jnp.float32),
        precision=lax.Precision.HIGHEST,
    )
    return (residual.astype(jnp.float32) + combined).astype(jnp.bfloat16)


def expert_kernel(count, *refs):
    blocks, (gain_ref, gate_ref, up_ref, down_ref) = refs[:count], refs[count : count + 4]
    mine_ref, theirs_ref, normed_ref = refs[count + 4 :]
    rows = blocks[0].shape[0]
    for i, block in enumerate(blocks):
        x = block[...].astype(jnp.float32)
        scale = lax.rsqrt(jnp.mean(x * x, axis=-1, keepdims=True) + 1e-05)
        normed_ref[pl.ds(i * rows, rows), :] = (x * scale * gain_ref[...]).astype(jnp.bfloat16)
    normed = normed_ref[...]
    across = (((1,), (1,)), ((), ()))
    gate = lax.dot_general(normed, gate_ref[...], across, preferred_element_type=jnp.float32)
    upper = lax.dot_general(normed, up_ref[...], across, preferred_element_type=jnp.float32)
    act = (gate * jax.nn.sigmoid(1.702 * gate) * (upper + 1.0)).astype(jnp.bfloat16)
    out = jnp.dot(act, down_ref[...], preferred_element_type=jnp.float32).astype(jnp.bfloat16)
    half = rows * (count // 2)
    mine_ref[...] = out[:half]
    theirs_ref[...] = out[half:]


def expert_parts(blocks, gain, gate_w, up_w, down_w):
    count = len(blocks)
    rows, model = blocks[0].shape
    out = jax.ShapeDtypeStruct((rows * count // 2, model), jnp.bfloat16)
    vmem = pl.BlockSpec(memory_space=pltpu.VMEM)
    hidden = gate_w.shape[0]
    return pl.pallas_call(
        functools.partial(expert_kernel, count),
        out_shape=(out, out),
        in_specs=[vmem] * (count + 4),
        out_specs=(vmem, vmem),
        scratch_shapes=[pltpu.VMEM((rows * count, model), jnp.bfloat16)],
        cost_estimate=pl.CostEstimate(
            flops=6 * rows * count * model * hidden,
            bytes_accessed=6 * model * hidden,
            transcendentals=rows * count * hidden,
        ),
        compiler_params=pltpu.CompilerParams(vmem_limit_bytes=24 * 2**20),
    )(*blocks, gain, gate_w, up_w, down_w)


def load_kernel(count, *refs):
    sources, targets, sems = refs[:count], refs[count : 2 * count], refs[2 * count]
    copies = [
        pltpu.make_async_copy(source, target, sems.at[i])
        for i, (source, target) in enumerate(zip(sources, targets))
    ]
    for copy in copies:
        copy.start()
    for copy in copies:
        copy.wait()


def load(*arrays):
    count = len(arrays)
    return pl.pallas_call(
        functools.partial(load_kernel, count),
        out_shape=tuple(pltpu.VMEM(a.shape, a.dtype) for a in arrays),
        in_specs=[pl.BlockSpec(memory_space=pltpu.HBM)] * count,
        out_specs=(pl.BlockSpec(memory_space=pltpu.VMEM),) * count,
        scratch_shapes=[pltpu.SemaphoreType.DMA((count,))],
        cost_estimate=pl.CostEstimate(
            flops=0, bytes_accessed=2 * sum(a.size * a.dtype.itemsize for a in arrays), transcendentals=0
        ),
        compiler_params=pltpu.CompilerParams(vmem_limit_bytes=16 * 2**20),
    )(*(pltpu.with_memory_space_constraint(a, pltpu.HBM) for a in arrays))


def halves(residual, norm_gain, expert_ids, expert_weights, gate_proj, up_proj, down_proj):
    rows, model = residual.shape
    chips = lax.axis_size("expert") // 2
    half = chips // 2
    gain = norm_gain.reshape(1, model)

    def across(value, mask):
        pairs = [(i, i ^ (2 * mask)) for i in range(2 * chips)]
        return lax.ppermute(value, "expert", pairs) if mask else value

    def swap(value):
        return partner(value, "expert", 0)

    x = residual
    mirrored = across(x, half)
    near = [across(x, mask) for mask in range(half)]
    near += [swap(block) for block in near]
    held = load(gate_proj[0].T, up_proj[0].T, down_proj[0])
    far = [across(mirrored, mask) for mask in range(half)]
    far += [swap(block) for block in far]

    expert = (lax.axis_index("expert") // 2) ^ jnp.arange(chips, dtype=jnp.int32)
    weights = jnp.sum(
        jnp.where(expert_ids[:, :, None] == expert[None, None, :], expert_weights[:, :, None], 0.0), axis=1
    )
    mirror_weights = across(weights[:, half:], half)

    def mix(blocks, block_weights):
        mine, theirs = expert_parts(blocks, gain, *held)
        done = pair_sum(mine, swap(theirs)).reshape(half, rows, model)
        total = jnp.zeros((rows, model), jnp.float32)
        for mask in range(half):
            total += block_weights[:, mask][:, None] * across(done[mask], mask).astype(jnp.float32)
        return total

    own = mix(near, weights[:, :half])
    other = mix(far, mirror_weights)
    own += across(other.astype(jnp.bfloat16), half).astype(jnp.float32)
    return (x.astype(jnp.float32) + own).astype(jnp.bfloat16)


def body(residual, norm_gain, expert_ids, expert_weights, gate_proj, up_proj, down_proj):
    rows, chosen = expert_ids.shape
    chips = lax.axis_size("expert") // 2
    whole = 2 * rows * chosen // chips >= rows and chips >= 4 and chips & (chips - 1) == 0
    plan = halves if whole else slots
    return plan(residual, norm_gain, expert_ids, expert_weights, gate_proj, up_proj, down_proj)


def solution(mesh):
    in_specs = (
        P(("groups", "expert"), None),
        P(),
        P(("groups", "expert"), None),
        P(("groups", "expert"), None),
        P("expert", None, None),
        P("expert", None, None),
        P("expert", None, None),
    )
    out_specs = P(("groups", "expert"), None)
    return jax.shard_map(body, mesh=mesh, in_specs=in_specs, out_specs=out_specs, check_vma=False)
```

```python
import functools

import jax
import jax.numpy as jnp
from jax import lax
from jax.experimental import pallas as pl
from jax.experimental.pallas import tpu as pltpu
from jax.sharding import PartitionSpec as P


def partner(value, axis, bit):
    mask = 2**bit
    pairs = [(source, source ^ mask) for source in range(lax.axis_size(axis))]
    return lax.ppermute(value, axis, pairs)


def expert_half(flat, gate_w, up_w, down_w):
    gate = jnp.dot(flat, gate_w, preferred_element_type=jnp.float32)
    upper = jnp.dot(flat, up_w, preferred_element_type=jnp.float32)
    act = (gate * jax.nn.sigmoid(1.702 * gate) * (upper + 1.0)).astype(jnp.bfloat16)
    return jnp.dot(act, down_w, preferred_element_type=jnp.float32).astype(jnp.bfloat16)


def normalised(rows, norm_gain):
    x = rows.astype(jnp.float32)
    scale = lax.rsqrt(jnp.mean(x * x, axis=-1, keepdims=True) + 1e-05)
    return (x * scale * norm_gain).astype(jnp.bfloat16)


def pair_sum(mine, theirs):
    return (mine.astype(jnp.float32) + theirs.astype(jnp.float32)).astype(jnp.bfloat16)


def slots(residual, norm_gain, expert_ids, expert_weights, gate_proj, up_proj, down_proj):
    rows, model = residual.shape
    chosen = expert_ids.shape[1]
    devices = lax.axis_size("expert")
    experts = devices // 2
    capacity = 2 * rows * chosen // experts
    half_cap = capacity // 2
    gate_w, up_w, down_w = (gate_proj[0], up_proj[0], down_proj[0])
    normed = normalised(residual, norm_gain)
    flat_ids = expert_ids.reshape(rows * chosen)
    onehot = (
        flat_ids[:, None] == lax.broadcasted_iota(jnp.int32, (rows * chosen, experts), 1)
    ).astype(jnp.int32)
    slot = jnp.sum(onehot * jnp.cumsum(onehot, axis=0), axis=1) - 1
    position = flat_ids * capacity + slot
    pick = (
        position[:, None] == lax.broadcasted_iota(jnp.int32, (rows * chosen, experts * capacity), 1)
    ).astype(jnp.float32)
    place_rows = jnp.sum(pick.reshape(rows, chosen, experts * capacity), axis=1)
    send = lax.dot_general(
        place_rows.astype(jnp.bfloat16),
        normed,
        (((0,), (0,)), ((), ())),
        preferred_element_type=jnp.float32,
    )
    outgoing = send.astype(jnp.bfloat16).reshape(devices, half_cap, model)
    arrived = lax.all_to_all(outgoing, "expert", split_axis=0, concat_axis=0, tiled=True)
    other = partner(arrived, "expert", 0)
    both = jnp.stack((arrived, other)).reshape(2 * devices * half_cap, model)
    both = expert_half(both, gate_w, up_w, down_w).reshape(2, devices, half_cap, model)
    returned = partner(both[1], "expert", 0)
    finished = pair_sum(both[0], returned)
    back = lax.all_to_all(finished, "expert", split_axis=0, concat_axis=0, tiled=True)
    weighted = jnp.sum(
        (pick * expert_weights.reshape(rows * chosen)[:, None]).reshape(
            rows, chosen, experts * capacity
        ),
        axis=1,
    )
    combined = jnp.dot(
        weighted,
        back.reshape(experts * capacity, model).astype(jnp.float32),
        precision=lax.Precision.HIGHEST,
    )
    return (residual.astype(jnp.float32) + combined).astype(jnp.bfloat16)


def expert_kernel(groups, *refs):
    count = sum(groups)
    blocks, (gain_ref, gate_ref, up_ref, down_ref, table_ref) = refs[:count], refs[count : count + 5]
    outs, table_out_ref, normed_ref = refs[count + 5 : -2], refs[-2], refs[-1]
    table_out_ref[...] = table_ref[...]
    rows, model = blocks[0].shape
    gain = gain_ref[...].reshape(1, model)
    for i, block in enumerate(blocks):
        x = block[...].astype(jnp.float32)
        scale = lax.rsqrt(jnp.mean(x * x, axis=-1, keepdims=True) + 1e-05)
        normed_ref[pl.ds(i * rows, rows), :] = (x * scale * gain).astype(jnp.bfloat16)
    normed = normed_ref[...]
    across = (((1,), (1,)), ((), ()))
    gate = lax.dot_general(normed, gate_ref[...], across, preferred_element_type=jnp.float32)
    upper = lax.dot_general(normed, up_ref[...], across, preferred_element_type=jnp.float32)
    act = (gate * jax.nn.sigmoid(1.702 * gate) * (upper + 1.0)).astype(jnp.bfloat16)
    out = jnp.dot(act, down_ref[...], preferred_element_type=jnp.float32).astype(jnp.bfloat16)
    start = 0
    for size, out_ref in zip(groups, outs):
        out_ref[...] = out[start * rows : (start + size) * rows]
        start += size


def expert_parts(groups, gain, gate_w, up_w, down_w, table):
    blocks = sum(groups, [])
    sizes = tuple(len(group) for group in groups)
    rows, model = blocks[0].shape
    count, hidden = len(blocks), gate_w.shape[0]
    vmem = pl.BlockSpec(memory_space=pltpu.VMEM)
    return pl.pallas_call(
        functools.partial(expert_kernel, sizes),
        out_shape=tuple(jax.ShapeDtypeStruct((rows * size, model), jnp.bfloat16) for size in sizes)
        + (jax.ShapeDtypeStruct(table.shape, table.dtype),),
        in_specs=[vmem] * (count + 5),
        out_specs=(vmem,) * (len(groups) + 1),
        scratch_shapes=[pltpu.VMEM((rows * count, model), jnp.bfloat16)],
        cost_estimate=pl.CostEstimate(
            flops=6 * rows * count * model * hidden,
            bytes_accessed=6 * model * hidden,
            transcendentals=rows * count * hidden,
        ),
        compiler_params=pltpu.CompilerParams(vmem_limit_bytes=24 * 2**20),
    )(*blocks, gain, gate_w, up_w, down_w, table)


def load_kernel(pieces, chip_ref, ids_ref, weights_ref, *refs):
    count = (len(refs) - 3) // 2
    sources, near_ref, far_ref = refs[:count], refs[count], refs[count + 1]
    targets, sems = refs[count + 2 : -1], refs[-1]
    copies = []
    for source, target in zip(sources, targets):
        part = source.shape[0] // pieces
        for piece in range(pieces):
            span = pl.ds(piece * part, part)
            copies.append(pltpu.make_async_copy(source.at[span], target.at[span], sems.at[len(copies)]))
    for copy in copies:
        copy.start()
    chosen, rows = ids_ref.shape
    half = near_ref.shape[1]
    expert = chip_ref[0] ^ lax.broadcasted_iota(jnp.int32, (2 * half, rows), 0)
    table = jnp.zeros((2 * half, rows), jnp.float32)
    for k in range(chosen):
        table += jnp.where(ids_ref[k : k + 1, :] == expert, weights_ref[k : k + 1, :], 0.0)
    near_ref[...] = table[:half].T
    far_ref[...] = table[half:].T
    for copy in copies:
        copy.wait()


def load(chip, expert_ids, expert_weights, half, arrays):
    rows = expert_ids.shape[0]
    pieces = 3 if all(a.shape[0] % 48 == 0 for a in arrays) else 1
    vmem = pl.BlockSpec(memory_space=pltpu.VMEM)
    table = jax.ShapeDtypeStruct((rows, half), jnp.float32)
    return pl.pallas_call(
        functools.partial(load_kernel, pieces),
        out_shape=(table, table) + tuple(pltpu.VMEM(a.shape, a.dtype) for a in arrays),
        in_specs=[pl.BlockSpec(memory_space=pltpu.SMEM), vmem, vmem]
        + [pl.BlockSpec(memory_space=pltpu.HBM)] * len(arrays),
        out_specs=(vmem,) * (2 + len(arrays)),
        scratch_shapes=[pltpu.SemaphoreType.DMA((pieces * len(arrays),))],
        cost_estimate=pl.CostEstimate(
            flops=0, bytes_accessed=2 * sum(a.size * a.dtype.itemsize for a in arrays), transcendentals=0
        ),
        compiler_params=pltpu.CompilerParams(vmem_limit_bytes=16 * 2**20),
    )(
        chip.reshape(1),
        expert_ids.T,
        expert_weights.T,
        *(pltpu.with_memory_space_constraint(a, pltpu.HBM) for a in arrays),
    )


def halves(residual, norm_gain, expert_ids, expert_weights, gate_proj, up_proj, down_proj):
    rows, model = residual.shape
    chips = lax.axis_size("expert") // 2
    half = chips // 2

    def across(value, mask):
        pairs = [(i, i ^ (2 * mask)) for i in range(2 * chips)]
        return lax.ppermute(value, "expert", pairs) if mask else value

    def swap(value):
        return partner(value, "expert", 0)

    x = residual
    mirrored = across(x, half)
    near = [across(x, mask) for mask in range(1, half)]
    near_swapped = [swap(x)]
    chip = lax.axis_index("expert") // 2
    near_weights, far_weights, *held = load(
        chip, expert_ids, expert_weights, half, (gate_proj[0].T, up_proj[0].T, down_proj[0])
    )
    near_weights, far_weights, *near = lax.optimization_barrier((near_weights, far_weights, *near))
    near_swapped += [swap(block) for block in near]
    far = [across(mirrored, mask) for mask in range(1, half)]
    far_swapped = [swap(mirrored)] + [swap(block) for block in far]
    *parts, mirror_weights = expert_parts(
        (far_swapped, [mirrored] + far, near_swapped, [x] + near), norm_gain, *held, across(far_weights, half)
    )

    def mix(theirs, mine, block_weights):
        done = pair_sum(mine, swap(theirs)).reshape(half, rows, model)
        total = jnp.zeros((rows, model), jnp.float32)
        for mask in range(half):
            total += block_weights[:, mask][:, None] * across(done[mask], mask).astype(jnp.float32)
        return total

    other = mix(parts[0], parts[1], mirror_weights)
    own = mix(parts[2], parts[3], near_weights)
    own += across(other.astype(jnp.bfloat16), half).astype(jnp.float32)
    return (x.astype(jnp.float32) + own).astype(jnp.bfloat16)


def body(residual, norm_gain, expert_ids, expert_weights, gate_proj, up_proj, down_proj):
    rows, chosen = expert_ids.shape
    chips = lax.axis_size("expert") // 2
    whole = 2 * rows * chosen // chips >= rows and chips >= 4 and chips & (chips - 1) == 0
    plan = halves if whole else slots
    return plan(residual, norm_gain, expert_ids, expert_weights, gate_proj, up_proj, down_proj)


def solution(mesh):
    in_specs = (
        P(("groups", "expert"), None),
        P(),
        P(("groups", "expert"), None),
        P(("groups", "expert"), None),
        P("expert", None, None),
        P("expert", None, None),
        P("expert", None, None),
    )
    out_specs = P(("groups", "expert"), None)
    return jax.shard_map(body, mesh=mesh, in_specs=in_specs, out_specs=out_specs, check_vma=False)
```

```python
import functools

import jax
import jax.numpy as jnp
from jax import lax
from jax.experimental import pallas as pl
from jax.experimental.pallas import tpu as pltpu
from jax.sharding import PartitionSpec as P


def partner(value, axis, bit):
    mask = 2**bit
    pairs = [(source, source ^ mask) for source in range(lax.axis_size(axis))]
    return lax.ppermute(value, axis, pairs)


def expert_half(flat, gate_w, up_w, down_w):
    gate = jnp.dot(flat, gate_w, preferred_element_type=jnp.float32)
    upper = jnp.dot(flat, up_w, preferred_element_type=jnp.float32)
    act = (gate * jax.nn.sigmoid(1.702 * gate) * (upper + 1.0)).astype(jnp.bfloat16)
    return jnp.dot(act, down_w, preferred_element_type=jnp.float32).astype(jnp.bfloat16)


def normalised(rows, norm_gain):
    x = rows.astype(jnp.float32)
    scale = lax.rsqrt(jnp.mean(x * x, axis=-1, keepdims=True) + 1e-05)
    return (x * scale * norm_gain).astype(jnp.bfloat16)


def pair_sum(mine, theirs):
    return (mine.astype(jnp.float32) + theirs.astype(jnp.float32)).astype(jnp.bfloat16)


def slots(residual, norm_gain, expert_ids, expert_weights, gate_proj, up_proj, down_proj):
    rows, model = residual.shape
    chosen = expert_ids.shape[1]
    devices = lax.axis_size("expert")
    experts = devices // 2
    capacity = 2 * rows * chosen // experts
    half_cap = capacity // 2
    gate_w, up_w, down_w = (gate_proj[0], up_proj[0], down_proj[0])
    normed = normalised(residual, norm_gain)
    flat_ids = expert_ids.reshape(rows * chosen)
    onehot = (
        flat_ids[:, None] == lax.broadcasted_iota(jnp.int32, (rows * chosen, experts), 1)
    ).astype(jnp.int32)
    slot = jnp.sum(onehot * jnp.cumsum(onehot, axis=0), axis=1) - 1
    position = flat_ids * capacity + slot
    pick = (
        position[:, None] == lax.broadcasted_iota(jnp.int32, (rows * chosen, experts * capacity), 1)
    ).astype(jnp.float32)
    place_rows = jnp.sum(pick.reshape(rows, chosen, experts * capacity), axis=1)
    send = lax.dot_general(
        place_rows.astype(jnp.bfloat16),
        normed,
        (((0,), (0,)), ((), ())),
        preferred_element_type=jnp.float32,
    )
    outgoing = send.astype(jnp.bfloat16).reshape(devices, half_cap, model)
    arrived = lax.all_to_all(outgoing, "expert", split_axis=0, concat_axis=0, tiled=True)
    other = partner(arrived, "expert", 0)
    both = jnp.stack((arrived, other)).reshape(2 * devices * half_cap, model)
    both = expert_half(both, gate_w, up_w, down_w).reshape(2, devices, half_cap, model)
    returned = partner(both[1], "expert", 0)
    finished = pair_sum(both[0], returned)
    back = lax.all_to_all(finished, "expert", split_axis=0, concat_axis=0, tiled=True)
    weighted = jnp.sum(
        (pick * expert_weights.reshape(rows * chosen)[:, None]).reshape(
            rows, chosen, experts * capacity
        ),
        axis=1,
    )
    combined = jnp.dot(
        weighted,
        back.reshape(experts * capacity, model).astype(jnp.float32),
        precision=lax.Precision.HIGHEST,
    )
    return (residual.astype(jnp.float32) + combined).astype(jnp.bfloat16)


def expert_kernel(groups, *refs):
    count = sum(groups)
    blocks, (gain_ref, gate_ref, up_hbm, down_hbm, table_ref) = refs[:count], refs[count : count + 5]
    outs, (table_out_ref, normed_ref, up_ref, down_ref, sems) = refs[count + 5 : -5], refs[-5:]
    up_copy = pltpu.make_async_copy(up_hbm, up_ref, sems.at[0])
    down_copy = pltpu.make_async_copy(down_hbm, down_ref, sems.at[1])
    up_copy.start()
    down_copy.start()
    table_out_ref[...] = table_ref[...]
    rows, model = blocks[0].shape
    gain = gain_ref[...].reshape(1, model)
    for i, block in enumerate(blocks):
        x = block[...].astype(jnp.float32)
        scale = lax.rsqrt(jnp.mean(x * x, axis=-1, keepdims=True) + 1e-05)
        normed_ref[pl.ds(i * rows, rows), :] = (x * scale * gain).astype(jnp.bfloat16)
    normed = normed_ref[...]
    across = (((1,), (1,)), ((), ()))
    gate = lax.dot_general(normed, gate_ref[...], across, preferred_element_type=jnp.float32)
    gate = gate * jax.nn.sigmoid(1.702 * gate)
    up_copy.wait()
    upper = lax.dot_general(normed, up_ref[...], across, preferred_element_type=jnp.float32)
    act = (gate * (upper + 1.0)).astype(jnp.bfloat16)
    down_copy.wait()
    out = jnp.dot(act, down_ref[...], preferred_element_type=jnp.float32).astype(jnp.bfloat16)
    start = 0
    for size, out_ref in zip(groups, outs):
        out_ref[...] = out[start * rows : (start + size) * rows]
        start += size


def expert_parts(groups, gain, gate_w, up_w, down_w, table):
    blocks = sum(groups, [])
    sizes = tuple(len(group) for group in groups)
    rows, model = blocks[0].shape
    count, hidden = len(blocks), gate_w.shape[0]
    vmem, hbm = pl.BlockSpec(memory_space=pltpu.VMEM), pl.BlockSpec(memory_space=pltpu.HBM)
    return pl.pallas_call(
        functools.partial(expert_kernel, sizes),
        out_shape=tuple(jax.ShapeDtypeStruct((rows * size, model), jnp.bfloat16) for size in sizes)
        + (jax.ShapeDtypeStruct(table.shape, table.dtype),),
        in_specs=[vmem] * (count + 2) + [hbm, hbm, vmem],
        out_specs=(vmem,) * (len(groups) + 1),
        scratch_shapes=[
            pltpu.VMEM((rows * count, model), jnp.bfloat16),
            pltpu.VMEM(up_w.shape, up_w.dtype),
            pltpu.VMEM(down_w.shape, down_w.dtype),
            pltpu.SemaphoreType.DMA((2,)),
        ],
        cost_estimate=pl.CostEstimate(
            flops=6 * rows * count * model * hidden,
            bytes_accessed=6 * model * hidden,
            transcendentals=rows * count * hidden,
        ),
        compiler_params=pltpu.CompilerParams(vmem_limit_bytes=32 * 2**20),
    )(
        *blocks,
        gain,
        gate_w,
        *(pltpu.with_memory_space_constraint(w, pltpu.HBM) for w in (up_w, down_w)),
        table,
    )


def load_kernel(chip_ref, ids_hbm, weights_hbm, source, near_ref, far_ref, target, ids_ref, weights_ref, sems):
    copies = [
        pltpu.make_async_copy(a, b, sems.at[i])
        for i, (a, b) in enumerate(((ids_hbm, ids_ref), (weights_hbm, weights_ref), (source, target)))
    ]
    for copy in copies:
        copy.start()
    chosen, rows = ids_ref.shape
    half = near_ref.shape[1]
    expert = chip_ref[0] ^ lax.broadcasted_iota(jnp.int32, (2 * half, rows), 0)
    copies[0].wait()
    copies[1].wait()
    table = jnp.zeros((2 * half, rows), jnp.float32)
    for k in range(chosen):
        table += jnp.where(ids_ref[k : k + 1, :] == expert, weights_ref[k : k + 1, :], 0.0)
    near_ref[...] = table[:half].T
    far_ref[...] = table[half:].T
    copies[2].wait()


def load(chip, expert_ids, expert_weights, half, array):
    rows, chosen = expert_ids.shape
    vmem, hbm = pl.BlockSpec(memory_space=pltpu.VMEM), pl.BlockSpec(memory_space=pltpu.HBM)
    table = jax.ShapeDtypeStruct((rows, half), jnp.float32)
    return pl.pallas_call(
        load_kernel,
        out_shape=(table, table, pltpu.VMEM(array.shape, array.dtype)),
        in_specs=[pl.BlockSpec(memory_space=pltpu.SMEM), hbm, hbm, hbm],
        out_specs=(vmem,) * 3,
        scratch_shapes=[
            pltpu.VMEM((chosen, rows), expert_ids.dtype),
            pltpu.VMEM((chosen, rows), expert_weights.dtype),
            pltpu.SemaphoreType.DMA((3,)),
        ],
        cost_estimate=pl.CostEstimate(
            flops=0, bytes_accessed=2 * array.size * array.dtype.itemsize, transcendentals=0
        ),
        compiler_params=pltpu.CompilerParams(vmem_limit_bytes=16 * 2**20),
    )(
        chip.reshape(1),
        *(pltpu.with_memory_space_constraint(a, pltpu.HBM) for a in (expert_ids.T, expert_weights.T, array)),
    )


def halves(residual, norm_gain, expert_ids, expert_weights, gate_proj, up_proj, down_proj):
    rows, model = residual.shape
    chips = lax.axis_size("expert") // 2
    half = chips // 2

    def across(value, mask):
        pairs = [(i, i ^ (2 * mask)) for i in range(2 * chips)]
        return lax.ppermute(value, "expert", pairs) if mask else value

    def swap(value):
        return partner(value, "expert", 0)

    x = residual
    mirrored = across(x, half)
    near = [across(x, mask) for mask in range(1, half)]
    near_swapped = [swap(x)]
    chip = lax.axis_index("expert") // 2
    near_weights, far_weights, gate_w = load(chip, expert_ids, expert_weights, half, gate_proj[0].T)
    near_weights, far_weights, *near = lax.optimization_barrier((near_weights, far_weights, *near))
    near_swapped += [swap(block) for block in near]
    far = [across(mirrored, mask) for mask in range(1, half)]
    far_swapped = [swap(mirrored)] + [swap(block) for block in far]
    *parts, mirror_weights = expert_parts(
        (far_swapped, [mirrored] + far, near_swapped, [x] + near),
        norm_gain,
        gate_w,
        up_proj[0].T,
        down_proj[0],
        across(far_weights, half),
    )

    def mix(done, block_weights):
        done = done.reshape(half, rows, model)
        total = jnp.zeros((rows, model), jnp.float32)
        for mask in range(half):
            total += block_weights[:, mask][:, None] * across(done[mask], mask).astype(jnp.float32)
        return total

    other = mix(pair_sum(parts[1], swap(parts[0])), mirror_weights).astype(jnp.bfloat16)
    near_done = pair_sum(parts[3], swap(parts[2]))
    other, near_done = lax.optimization_barrier((other, near_done))
    own = across(other, half).astype(jnp.float32) + mix(near_done, near_weights)
    return (x.astype(jnp.float32) + own).astype(jnp.bfloat16)


def body(residual, norm_gain, expert_ids, expert_weights, gate_proj, up_proj, down_proj):
    rows, chosen = expert_ids.shape
    chips = lax.axis_size("expert") // 2
    whole = 2 * rows * chosen // chips >= rows and chips >= 4 and chips & (chips - 1) == 0
    plan = halves if whole else slots
    return plan(residual, norm_gain, expert_ids, expert_weights, gate_proj, up_proj, down_proj)


def solution(mesh):
    in_specs = (
        P(("groups", "expert"), None),
        P(),
        P(("groups", "expert"), None),
        P(("groups", "expert"), None),
        P("expert", None, None),
        P("expert", None, None),
        P("expert", None, None),
    )
    out_specs = P(("groups", "expert"), None)
    return jax.shard_map(body, mesh=mesh, in_specs=in_specs, out_specs=out_specs, check_vma=False)
```

```python
import functools

import jax
import jax.numpy as jnp
from jax import lax
from jax.experimental import pallas as pl
from jax.experimental.pallas import tpu as pltpu
from jax.sharding import PartitionSpec as P


def partner(value, axis, bit):
    mask = 2**bit
    pairs = [(source, source ^ mask) for source in range(lax.axis_size(axis))]
    return lax.ppermute(value, axis, pairs)


def expert_half(flat, gate_w, up_w, down_w):
    gate = jnp.dot(flat, gate_w, preferred_element_type=jnp.float32)
    upper = jnp.dot(flat, up_w, preferred_element_type=jnp.float32)
    act = (gate * jax.nn.sigmoid(1.702 * gate) * (upper + 1.0)).astype(jnp.bfloat16)
    return jnp.dot(act, down_w, preferred_element_type=jnp.float32).astype(jnp.bfloat16)


def normalised(rows, norm_gain):
    x = rows.astype(jnp.float32)
    scale = lax.rsqrt(jnp.mean(x * x, axis=-1, keepdims=True) + 1e-05)
    return (x * scale * norm_gain).astype(jnp.bfloat16)


def pair_sum(mine, theirs):
    return (mine.astype(jnp.float32) + theirs.astype(jnp.float32)).astype(jnp.bfloat16)


def slots(residual, norm_gain, expert_ids, expert_weights, gate_proj, up_proj, down_proj):
    rows, model = residual.shape
    chosen = expert_ids.shape[1]
    devices = lax.axis_size("expert")
    experts = devices // 2
    capacity = 2 * rows * chosen // experts
    half_cap = capacity // 2
    gate_w, up_w, down_w = (gate_proj[0], up_proj[0], down_proj[0])
    normed = normalised(residual, norm_gain)
    flat_ids = expert_ids.reshape(rows * chosen)
    onehot = (
        flat_ids[:, None] == lax.broadcasted_iota(jnp.int32, (rows * chosen, experts), 1)
    ).astype(jnp.int32)
    slot = jnp.sum(onehot * jnp.cumsum(onehot, axis=0), axis=1) - 1
    position = flat_ids * capacity + slot
    pick = (
        position[:, None] == lax.broadcasted_iota(jnp.int32, (rows * chosen, experts * capacity), 1)
    ).astype(jnp.float32)
    place_rows = jnp.sum(pick.reshape(rows, chosen, experts * capacity), axis=1)
    send = lax.dot_general(
        place_rows.astype(jnp.bfloat16),
        normed,
        (((0,), (0,)), ((), ())),
        preferred_element_type=jnp.float32,
    )
    outgoing = send.astype(jnp.bfloat16).reshape(devices, half_cap, model)
    arrived = lax.all_to_all(outgoing, "expert", split_axis=0, concat_axis=0, tiled=True)
    other = partner(arrived, "expert", 0)
    both = jnp.stack((arrived, other)).reshape(2 * devices * half_cap, model)
    both = expert_half(both, gate_w, up_w, down_w).reshape(2, devices, half_cap, model)
    returned = partner(both[1], "expert", 0)
    finished = pair_sum(both[0], returned)
    back = lax.all_to_all(finished, "expert", split_axis=0, concat_axis=0, tiled=True)
    weighted = jnp.sum(
        (pick * expert_weights.reshape(rows * chosen)[:, None]).reshape(
            rows, chosen, experts * capacity
        ),
        axis=1,
    )
    combined = jnp.dot(
        weighted,
        back.reshape(experts * capacity, model).astype(jnp.float32),
        precision=lax.Precision.HIGHEST,
    )
    return (residual.astype(jnp.float32) + combined).astype(jnp.bfloat16)


def pack_kernel(after, *refs):
    refs = refs[after:]
    blocks, gain_ref, out_ref = refs[:-2], refs[-2], refs[-1]
    rows, model = blocks[0].shape
    gain = gain_ref[...].reshape(1, model)
    for i, block in enumerate(blocks):
        x = block[...].astype(jnp.float32)
        scale = lax.rsqrt(jnp.mean(x * x, axis=-1, keepdims=True) + 1e-05)
        out_ref[pl.ds(i * rows, rows), :] = (x * scale * gain).astype(jnp.bfloat16)


def pack(blocks, gain, after=()):
    rows, model = blocks[0].shape
    vmem = pl.BlockSpec(memory_space=pltpu.VMEM)
    return pl.pallas_call(
        functools.partial(pack_kernel, len(after)),
        out_shape=jax.ShapeDtypeStruct((rows * len(blocks), model), jnp.bfloat16),
        in_specs=[pl.BlockSpec(memory_space=pl.ANY)] * len(after) + [vmem] * (len(blocks) + 1),
        out_specs=vmem,
        compiler_params=pltpu.CompilerParams(vmem_limit_bytes=8 * 2**20),
    )(*after, *blocks, gain)


def mix_kernel(table_ref, *refs):
    blocks, out_ref = refs[:-1], refs[-1]
    total = jnp.zeros(out_ref.shape, jnp.float32)
    for i, block in enumerate(blocks):
        total += table_ref[:, i : i + 1] * block[...].astype(jnp.float32)
    out_ref[...] = total.astype(out_ref.dtype)


def mixed(table, blocks):
    vmem = pl.BlockSpec(memory_space=pltpu.VMEM)
    return pl.pallas_call(
        mix_kernel,
        out_shape=jax.ShapeDtypeStruct(blocks[0].shape, blocks[0].dtype),
        in_specs=[vmem] * (len(blocks) + 1),
        out_specs=vmem,
        compiler_params=pltpu.CompilerParams(vmem_limit_bytes=8 * 2**20),
    )(table, *blocks)


def expert_kernel(count, *refs):
    groups, (gate_ref, up_ref, down_ref, table_ref) = refs[:count], refs[count : count + 4]
    outs, table_out_ref, rows_ref = refs[count + 4 : -2], refs[-2], refs[-1]
    table_out_ref[...] = table_ref[...]
    rows = groups[0].shape[0]
    for i, group in enumerate(groups):
        rows_ref[pl.ds(i * rows, rows), :] = group[...]
    normed = rows_ref[...]
    across = (((1,), (1,)), ((), ()))
    gate = lax.dot_general(normed, gate_ref[...], across, preferred_element_type=jnp.float32)
    upper = lax.dot_general(normed, up_ref[...], across, preferred_element_type=jnp.float32)
    act = (gate * jax.nn.sigmoid(1.702 * gate) * (upper + 1.0)).astype(jnp.bfloat16)
    out = jnp.dot(act, down_ref[...], preferred_element_type=jnp.float32).astype(jnp.bfloat16)
    for i, out_ref in enumerate(outs):
        out_ref[...] = out[i * rows : (i + 1) * rows]


def expert_parts(groups, gate_w, up_w, down_w, table):
    count = len(groups)
    rows, model = groups[0].shape
    hidden = gate_w.shape[0]
    vmem = pl.BlockSpec(memory_space=pltpu.VMEM)
    return pl.pallas_call(
        functools.partial(expert_kernel, count),
        out_shape=(jax.ShapeDtypeStruct((rows, model), jnp.bfloat16),) * count
        + (jax.ShapeDtypeStruct(table.shape, table.dtype),),
        in_specs=[vmem] * (count + 4),
        out_specs=(vmem,) * (count + 1),
        scratch_shapes=[pltpu.VMEM((rows * count, model), jnp.bfloat16)],
        cost_estimate=pl.CostEstimate(
            flops=6 * rows * count * model * hidden,
            bytes_accessed=6 * model * hidden,
            transcendentals=rows * count * hidden,
        ),
        compiler_params=pltpu.CompilerParams(vmem_limit_bytes=24 * 2**20),
    )(*groups, gate_w, up_w, down_w, table)


def read_kernel(count, *refs):
    sources, targets = refs[1 : count + 1], refs[count + 1 : 2 * count + 1]
    token_ref, sems = refs[-2], refs[-1]
    copies = [
        pltpu.make_async_copy(source, target, sems.at[i])
        for i, (source, target) in enumerate(zip(sources, targets))
    ]
    for copy in copies:
        copy.start()
    token_ref[0] = 0
    for copy in copies:
        copy.wait()


def read(arrays, after):
    count = len(arrays)
    vmem, hbm = pl.BlockSpec(memory_space=pltpu.VMEM), pl.BlockSpec(memory_space=pltpu.HBM)
    return pl.pallas_call(
        functools.partial(read_kernel, count),
        out_shape=tuple(pltpu.VMEM(a.shape, a.dtype) for a in arrays)
        + (jax.ShapeDtypeStruct((1,), jnp.int32),),
        in_specs=[pl.BlockSpec(memory_space=pl.ANY)] + [hbm] * count,
        out_specs=(vmem,) * count + (pl.BlockSpec(memory_space=pltpu.SMEM),),
        scratch_shapes=[pltpu.SemaphoreType.DMA((count,))],
        cost_estimate=pl.CostEstimate(
            flops=0, bytes_accessed=2 * sum(a.size * a.dtype.itemsize for a in arrays), transcendentals=0
        ),
        compiler_params=pltpu.CompilerParams(vmem_limit_bytes=16 * 2**20),
    )(after, *(pltpu.with_memory_space_constraint(a, pltpu.HBM) for a in arrays))


def load_kernel(chip_ref, ids_hbm, weights_hbm, source, near_ref, far_ref, target, ids_ref, weights_ref, sems):
    copies = [
        pltpu.make_async_copy(a, b, sems.at[i])
        for i, (a, b) in enumerate(((ids_hbm, ids_ref), (weights_hbm, weights_ref), (source, target)))
    ]
    for copy in copies:
        copy.start()
    chosen, rows = ids_ref.shape
    half = near_ref.shape[1]
    expert = chip_ref[0] ^ lax.broadcasted_iota(jnp.int32, (2 * half, rows), 0)
    copies[0].wait()
    copies[1].wait()
    table = jnp.zeros((2 * half, rows), jnp.float32)
    for k in range(chosen):
        table += jnp.where(ids_ref[k : k + 1, :] == expert, weights_ref[k : k + 1, :], 0.0)
    near_ref[...] = table[:half].T
    far_ref[...] = table[half:].T
    copies[2].wait()


def load(chip, expert_ids, expert_weights, half, array):
    rows, chosen = expert_ids.shape
    vmem, hbm = pl.BlockSpec(memory_space=pltpu.VMEM), pl.BlockSpec(memory_space=pltpu.HBM)
    table = jax.ShapeDtypeStruct((rows, half), jnp.float32)
    return pl.pallas_call(
        load_kernel,
        out_shape=(table, table, pltpu.VMEM(array.shape, array.dtype)),
        in_specs=[pl.BlockSpec(memory_space=pltpu.SMEM), hbm, hbm, hbm],
        out_specs=(vmem,) * 3,
        scratch_shapes=[
            pltpu.VMEM((chosen, rows), expert_ids.dtype),
            pltpu.VMEM((chosen, rows), expert_weights.dtype),
            pltpu.SemaphoreType.DMA((3,)),
        ],
        cost_estimate=pl.CostEstimate(
            flops=0, bytes_accessed=2 * array.size * array.dtype.itemsize, transcendentals=0
        ),
        compiler_params=pltpu.CompilerParams(vmem_limit_bytes=16 * 2**20),
    )(
        chip,
        *(pltpu.with_memory_space_constraint(a, pltpu.HBM) for a in (expert_ids.T, expert_weights.T, array)),
    )


def halves(residual, norm_gain, expert_ids, expert_weights, gate_proj, up_proj, down_proj):
    rows, model = residual.shape
    chips = lax.axis_size("expert") // 2
    half = chips // 2

    def across(value, mask):
        pairs = [(i, i ^ (2 * mask)) for i in range(2 * chips)]
        return lax.ppermute(value, "expert", pairs) if mask else value

    def swap(value):
        return partner(value, "expert", 0)

    x = residual
    mirrored = across(x, half)
    near = [across(x, mask) for mask in range(1, half)]
    chip = (lax.axis_index("expert") // 2).reshape(1)
    near_weights, far_weights, gate_w = load(chip, expert_ids, expert_weights, half, gate_proj[0].T)
    far = [across(mirrored, mask) for mask in range(1, half)]
    near_rows = pack([x] + near, norm_gain, (near_weights, mirrored))
    near_swapped = swap(near_rows)
    up_w, down_w, token = read((up_proj[0].T, down_proj[0]), near_swapped)
    far_rows = pack([mirrored] + far, norm_gain, (token,))
    groups = (swap(far_rows), far_rows, near_swapped, near_rows)
    *parts, far_weights = expert_parts(groups, gate_w, up_w, down_w, far_weights)
    mirror_weights = across(far_weights, half)

    def give_back(done):
        done = done.reshape(half, rows, model)
        return [across(done[mask], mask) for mask in range(half)]

    far_blocks = give_back(pair_sum(parts[1], swap(parts[0])))
    near_blocks = give_back(pair_sum(parts[3], swap(parts[2])))
    total = x.astype(jnp.float32) + across(mixed(mirror_weights, far_blocks), half).astype(jnp.float32)
    for mask, block in enumerate(near_blocks):
        total += near_weights[:, mask][:, None] * block.astype(jnp.float32)
    return total.astype(jnp.bfloat16)


def body(residual, norm_gain, expert_ids, expert_weights, gate_proj, up_proj, down_proj):
    rows, chosen = expert_ids.shape
    chips = lax.axis_size("expert") // 2
    whole = 2 * rows * chosen // chips >= rows and chips >= 4 and chips & (chips - 1) == 0
    plan = halves if whole else slots
    return plan(residual, norm_gain, expert_ids, expert_weights, gate_proj, up_proj, down_proj)


def solution(mesh):
    in_specs = (
        P(("groups", "expert"), None),
        P(),
        P(("groups", "expert"), None),
        P(("groups", "expert"), None),
        P("expert", None, None),
        P("expert", None, None),
        P("expert", None, None),
    )
    out_specs = P(("groups", "expert"), None)
    return jax.shard_map(body, mesh=mesh, in_specs=in_specs, out_specs=out_specs, check_vma=False)
```

```python
import functools

import jax
import jax.numpy as jnp
from jax import lax
from jax.experimental import pallas as pl
from jax.experimental.pallas import tpu as pltpu
from jax.sharding import PartitionSpec as P


def partner(value, axis, bit):
    mask = 2**bit
    pairs = [(source, source ^ mask) for source in range(lax.axis_size(axis))]
    return lax.ppermute(value, axis, pairs)


def expert_half(flat, gate_w, up_w, down_w):
    gate = jnp.dot(flat, gate_w, preferred_element_type=jnp.float32)
    upper = jnp.dot(flat, up_w, preferred_element_type=jnp.float32)
    act = (gate * jax.nn.sigmoid(1.702 * gate) * (upper + 1.0)).astype(jnp.bfloat16)
    return jnp.dot(act, down_w, preferred_element_type=jnp.float32).astype(jnp.bfloat16)


def normalised(rows, norm_gain):
    x = rows.astype(jnp.float32)
    scale = lax.rsqrt(jnp.mean(x * x, axis=-1, keepdims=True) + 1e-05)
    return (x * scale * norm_gain).astype(jnp.bfloat16)


def pair_sum(mine, theirs):
    return (mine.astype(jnp.float32) + theirs.astype(jnp.float32)).astype(jnp.bfloat16)


def slots(residual, norm_gain, expert_ids, expert_weights, gate_proj, up_proj, down_proj):
    rows, model = residual.shape
    chosen = expert_ids.shape[1]
    devices = lax.axis_size("expert")
    experts = devices // 2
    capacity = 2 * rows * chosen // experts
    half_cap = capacity // 2
    gate_w, up_w, down_w = (gate_proj[0], up_proj[0], down_proj[0])
    normed = normalised(residual, norm_gain)
    flat_ids = expert_ids.reshape(rows * chosen)
    onehot = (
        flat_ids[:, None] == lax.broadcasted_iota(jnp.int32, (rows * chosen, experts), 1)
    ).astype(jnp.int32)
    slot = jnp.sum(onehot * jnp.cumsum(onehot, axis=0), axis=1) - 1
    position = flat_ids * capacity + slot
    pick = (
        position[:, None] == lax.broadcasted_iota(jnp.int32, (rows * chosen, experts * capacity), 1)
    ).astype(jnp.float32)
    place_rows = jnp.sum(pick.reshape(rows, chosen, experts * capacity), axis=1)
    send = lax.dot_general(
        place_rows.astype(jnp.bfloat16),
        normed,
        (((0,), (0,)), ((), ())),
        preferred_element_type=jnp.float32,
    )
    outgoing = send.astype(jnp.bfloat16).reshape(devices, half_cap, model)
    arrived = lax.all_to_all(outgoing, "expert", split_axis=0, concat_axis=0, tiled=True)
    other = partner(arrived, "expert", 0)
    both = jnp.stack((arrived, other)).reshape(2 * devices * half_cap, model)
    both = expert_half(both, gate_w, up_w, down_w).reshape(2, devices, half_cap, model)
    returned = partner(both[1], "expert", 0)
    finished = pair_sum(both[0], returned)
    back = lax.all_to_all(finished, "expert", split_axis=0, concat_axis=0, tiled=True)
    weighted = jnp.sum(
        (pick * expert_weights.reshape(rows * chosen)[:, None]).reshape(
            rows, chosen, experts * capacity
        ),
        axis=1,
    )
    combined = jnp.dot(
        weighted,
        back.reshape(experts * capacity, model).astype(jnp.float32),
        precision=lax.Precision.HIGHEST,
    )
    return (residual.astype(jnp.float32) + combined).astype(jnp.bfloat16)


def pack_kernel(after, sizes, *refs):
    blocks, gain_ref, outs = refs[after : -1 - len(sizes)], refs[-1 - len(sizes)], refs[-len(sizes) :]
    rows, model = blocks[0].shape
    gain = gain_ref[...].reshape(1, model)
    places = [(out, i) for out, size in zip(outs, sizes) for i in range(size)]
    for block, (out_ref, i) in zip(blocks, places):
        x = block[...].astype(jnp.float32)
        scale = lax.rsqrt(jnp.mean(x * x, axis=-1, keepdims=True) + 1e-05)
        out_ref[pl.ds(i * rows, rows), :] = (x * scale * gain).astype(jnp.bfloat16)


def pack(groups, gain, after):
    blocks = sum(groups, [])
    sizes = tuple(len(group) for group in groups)
    rows, model = blocks[0].shape
    vmem = pl.BlockSpec(memory_space=pltpu.VMEM)
    return pl.pallas_call(
        functools.partial(pack_kernel, len(after), sizes),
        out_shape=tuple(jax.ShapeDtypeStruct((rows * size, model), jnp.bfloat16) for size in sizes),
        in_specs=[pl.BlockSpec(memory_space=pl.ANY)] * len(after) + [vmem] * (len(blocks) + 1),
        out_specs=(vmem,) * len(sizes),
        compiler_params=pltpu.CompilerParams(vmem_limit_bytes=8 * 2**20),
    )(*after, *blocks, gain)


def mix_kernel(table_ref, *refs):
    blocks, out_ref = refs[:-1], refs[-1]
    total = jnp.zeros(out_ref.shape, jnp.float32)
    for i, block in enumerate(blocks):
        total += table_ref[:, i : i + 1] * block[...].astype(jnp.float32)
    out_ref[...] = total.astype(out_ref.dtype)


def mixed(table, blocks):
    vmem = pl.BlockSpec(memory_space=pltpu.VMEM)
    return pl.pallas_call(
        mix_kernel,
        out_shape=jax.ShapeDtypeStruct(blocks[0].shape, blocks[0].dtype),
        in_specs=[vmem] * (len(blocks) + 1),
        out_specs=vmem,
        compiler_params=pltpu.CompilerParams(vmem_limit_bytes=8 * 2**20),
    )(table, *blocks)


def expert_kernel(count, *refs):
    groups, (gate_ref, up_ref, down_ref, table_ref) = refs[:count], refs[count : count + 4]
    outs, table_out_ref = refs[count + 4 : -1], refs[-1]
    table_out_ref[...] = table_ref[...]
    normed = jnp.concatenate([group[...] for group in groups])
    across = (((1,), (1,)), ((), ()))
    gate = lax.dot_general(normed, gate_ref[...], across, preferred_element_type=jnp.float32)
    upper = lax.dot_general(normed, up_ref[...], across, preferred_element_type=jnp.float32)
    act = (gate * jax.nn.sigmoid(1.702 * gate) * (upper + 1.0)).astype(jnp.bfloat16)
    out = jnp.dot(act, down_ref[...], preferred_element_type=jnp.float32).astype(jnp.bfloat16)
    start = 0
    for out_ref in outs:
        rows = out_ref.shape[0]
        out_ref[...] = out[start : start + rows]
        start += rows


def expert_parts(groups, sizes, gate_w, up_w, down_w, table):
    count, rows = len(groups), sum(sizes)
    hidden, model = gate_w.shape
    vmem = pl.BlockSpec(memory_space=pltpu.VMEM)
    return pl.pallas_call(
        functools.partial(expert_kernel, count),
        out_shape=tuple(jax.ShapeDtypeStruct((size, model), jnp.bfloat16) for size in sizes)
        + (jax.ShapeDtypeStruct(table.shape, table.dtype),),
        in_specs=[vmem] * (count + 4),
        out_specs=(vmem,) * (len(sizes) + 1),
        cost_estimate=pl.CostEstimate(
            flops=6 * rows * model * hidden, bytes_accessed=6 * model * hidden, transcendentals=rows * hidden
        ),
        compiler_params=pltpu.CompilerParams(vmem_limit_bytes=24 * 2**20),
    )(*groups, gate_w, up_w, down_w, table)


def read_kernel(after, *refs):
    refs, sems = refs[after:-1], refs[-1]
    sources, targets = refs[: len(refs) // 2], refs[len(refs) // 2 :]
    copies = [
        pltpu.make_async_copy(source, target, sems.at[i])
        for i, (source, target) in enumerate(zip(sources, targets))
    ]
    for copy in copies:
        copy.start()
    for copy in copies:
        copy.wait()


def read(arrays, after):
    count = len(arrays)
    vmem, hbm = pl.BlockSpec(memory_space=pltpu.VMEM), pl.BlockSpec(memory_space=pltpu.HBM)
    return pl.pallas_call(
        functools.partial(read_kernel, len(after)),
        out_shape=tuple(pltpu.VMEM(a.shape, a.dtype) for a in arrays),
        in_specs=[pl.BlockSpec(memory_space=pl.ANY)] * len(after) + [hbm] * count,
        out_specs=(vmem,) * count,
        scratch_shapes=[pltpu.SemaphoreType.DMA((count,))],
        cost_estimate=pl.CostEstimate(
            flops=0, bytes_accessed=2 * sum(a.size * a.dtype.itemsize for a in arrays), transcendentals=0
        ),
        compiler_params=pltpu.CompilerParams(vmem_limit_bytes=16 * 2**20),
    )(*after, *(pltpu.with_memory_space_constraint(a, pltpu.HBM) for a in arrays))


def load_kernel(chip_ref, ids_hbm, weights_hbm, source, near_ref, far_ref, target, ids_ref, weights_ref, sems):
    copies = [
        pltpu.make_async_copy(a, b, sems.at[i])
        for i, (a, b) in enumerate(((ids_hbm, ids_ref), (weights_hbm, weights_ref), (source, target)))
    ]
    for copy in copies:
        copy.start()
    chosen, rows = ids_ref.shape
    half = near_ref.shape[1]
    expert = chip_ref[0] ^ lax.broadcasted_iota(jnp.int32, (2 * half, rows), 0)
    copies[0].wait()
    copies[1].wait()
    table = jnp.zeros((2 * half, rows), jnp.float32)
    for k in range(chosen):
        table += jnp.where(ids_ref[k : k + 1, :] == expert, weights_ref[k : k + 1, :], 0.0)
    near_ref[...] = table[:half].T
    far_ref[...] = table[half:].T
    copies[2].wait()


def load(chip, expert_ids, expert_weights, half, array):
    rows, chosen = expert_ids.shape
    vmem, hbm = pl.BlockSpec(memory_space=pltpu.VMEM), pl.BlockSpec(memory_space=pltpu.HBM)
    table = jax.ShapeDtypeStruct((rows, half), jnp.float32)
    return pl.pallas_call(
        load_kernel,
        out_shape=(table, table, pltpu.VMEM(array.shape, array.dtype)),
        in_specs=[pl.BlockSpec(memory_space=pltpu.SMEM), hbm, hbm, hbm],
        out_specs=(vmem,) * 3,
        scratch_shapes=[
            pltpu.VMEM((chosen, rows), expert_ids.dtype),
            pltpu.VMEM((chosen, rows), expert_weights.dtype),
            pltpu.SemaphoreType.DMA((3,)),
        ],
        cost_estimate=pl.CostEstimate(
            flops=0, bytes_accessed=2 * array.size * array.dtype.itemsize, transcendentals=0
        ),
        compiler_params=pltpu.CompilerParams(vmem_limit_bytes=16 * 2**20),
    )(
        chip,
        *(pltpu.with_memory_space_constraint(a, pltpu.HBM) for a in (expert_ids.T, expert_weights.T, array)),
    )


def halves(residual, norm_gain, expert_ids, expert_weights, gate_proj, up_proj, down_proj):
    rows, model = residual.shape
    chips = lax.axis_size("expert") // 2
    half = chips // 2

    def across(value, mask):
        pairs = [(i, i ^ (2 * mask)) for i in range(2 * chips)]
        return lax.ppermute(value, "expert", pairs) if mask else value

    def swap(value):
        return partner(value, "expert", 0)

    x = residual
    mirrored = across(x, half)
    near = [across(x, mask) for mask in range(1, half)]
    chip = (lax.axis_index("expert") // 2).reshape(1)
    near_weights, far_weights, gate_w = load(chip, expert_ids, expert_weights, half, gate_proj[0].T)
    (mirrored,) = pack(([mirrored],), norm_gain, (near_weights,))
    far = [across(mirrored, mask) for mask in range(1, half)]
    mirror_swapped = swap(mirrored)
    up_w, down_w = read((up_proj[0].T, down_proj[0]), (mirror_swapped, *near))
    far_swapped = [swap(block) for block in far]
    (near_rows,) = pack(([x] + near,), norm_gain, (up_w, *far))
    *parts, far_weights = expert_parts(
        (mirror_swapped, *far_swapped, mirrored, *far, swap(near_rows), near_rows),
        (half * rows,) * 4,
        gate_w,
        up_w,
        down_w,
        far_weights,
    )
    mirror_weights = across(far_weights, half)

    def give_back(done):
        done = done.reshape(half, rows, model)
        return [across(done[mask], mask) for mask in range(half)]

    far_blocks = give_back(pair_sum(parts[1], swap(parts[0])))
    near_blocks = give_back(pair_sum(parts[3], swap(parts[2])))
    total = x.astype(jnp.float32) + across(mixed(mirror_weights, far_blocks), half).astype(jnp.float32)
    for mask, block in enumerate(near_blocks):
        total += near_weights[:, mask][:, None] * block.astype(jnp.float32)
    return total.astype(jnp.bfloat16)


def body(residual, norm_gain, expert_ids, expert_weights, gate_proj, up_proj, down_proj):
    rows, chosen = expert_ids.shape
    chips = lax.axis_size("expert") // 2
    whole = 2 * rows * chosen // chips >= rows and chips >= 4 and chips & (chips - 1) == 0
    plan = halves if whole else slots
    return plan(residual, norm_gain, expert_ids, expert_weights, gate_proj, up_proj, down_proj)


def solution(mesh):
    in_specs = (
        P(("groups", "expert"), None),
        P(),
        P(("groups", "expert"), None),
        P(("groups", "expert"), None),
        P("expert", None, None),
        P("expert", None, None),
        P("expert", None, None),
    )
    out_specs = P(("groups", "expert"), None)
    return jax.shard_map(body, mesh=mesh, in_specs=in_specs, out_specs=out_specs, check_vma=False)
```

```python
import functools

import jax
import jax.numpy as jnp
from jax import lax
from jax.experimental import pallas as pl
from jax.experimental.pallas import tpu as pltpu
from jax.sharding import PartitionSpec as P


def partner(value, axis, bit):
    mask = 2**bit
    pairs = [(source, source ^ mask) for source in range(lax.axis_size(axis))]
    return lax.ppermute(value, axis, pairs)


def expert_half(flat, gate_w, up_w, down_w):
    gate = jnp.dot(flat, gate_w, preferred_element_type=jnp.float32)
    upper = jnp.dot(flat, up_w, preferred_element_type=jnp.float32)
    act = (gate * jax.nn.sigmoid(1.702 * gate) * (upper + 1.0)).astype(jnp.bfloat16)
    return jnp.dot(act, down_w, preferred_element_type=jnp.float32).astype(jnp.bfloat16)


def normalised(rows, norm_gain):
    x = rows.astype(jnp.float32)
    scale = lax.rsqrt(jnp.mean(x * x, axis=-1, keepdims=True) + 1e-05)
    return (x * scale * norm_gain).astype(jnp.bfloat16)


def pair_sum(mine, theirs):
    return (mine.astype(jnp.float32) + theirs.astype(jnp.float32)).astype(jnp.bfloat16)


def slots(residual, norm_gain, expert_ids, expert_weights, gate_proj, up_proj, down_proj):
    rows, model = residual.shape
    chosen = expert_ids.shape[1]
    devices = lax.axis_size("expert")
    experts = devices // 2
    capacity = 2 * rows * chosen // experts
    half_cap = capacity // 2
    gate_w, up_w, down_w = (gate_proj[0], up_proj[0], down_proj[0])
    normed = normalised(residual, norm_gain)
    flat_ids = expert_ids.reshape(rows * chosen)
    onehot = (
        flat_ids[:, None] == lax.broadcasted_iota(jnp.int32, (rows * chosen, experts), 1)
    ).astype(jnp.int32)
    slot = jnp.sum(onehot * jnp.cumsum(onehot, axis=0), axis=1) - 1
    position = flat_ids * capacity + slot
    pick = (
        position[:, None] == lax.broadcasted_iota(jnp.int32, (rows * chosen, experts * capacity), 1)
    ).astype(jnp.float32)
    place_rows = jnp.sum(pick.reshape(rows, chosen, experts * capacity), axis=1)
    send = lax.dot_general(
        place_rows.astype(jnp.bfloat16),
        normed,
        (((0,), (0,)), ((), ())),
        preferred_element_type=jnp.float32,
    )
    outgoing = send.astype(jnp.bfloat16).reshape(devices, half_cap, model)
    arrived = lax.all_to_all(outgoing, "expert", split_axis=0, concat_axis=0, tiled=True)
    other = partner(arrived, "expert", 0)
    both = jnp.stack((arrived, other)).reshape(2 * devices * half_cap, model)
    both = expert_half(both, gate_w, up_w, down_w).reshape(2, devices, half_cap, model)
    returned = partner(both[1], "expert", 0)
    finished = pair_sum(both[0], returned)
    back = lax.all_to_all(finished, "expert", split_axis=0, concat_axis=0, tiled=True)
    weighted = jnp.sum(
        (pick * expert_weights.reshape(rows * chosen)[:, None]).reshape(
            rows, chosen, experts * capacity
        ),
        axis=1,
    )
    combined = jnp.dot(
        weighted,
        back.reshape(experts * capacity, model).astype(jnp.float32),
        precision=lax.Precision.HIGHEST,
    )
    return (residual.astype(jnp.float32) + combined).astype(jnp.bfloat16)


def pack_kernel(after, sizes, *refs):
    blocks, gain_ref, outs = refs[after : -1 - len(sizes)], refs[-1 - len(sizes)], refs[-len(sizes) :]
    rows, model = blocks[0].shape
    gain = gain_ref[...].reshape(1, model)
    places = [(out, i) for out, size in zip(outs, sizes) for i in range(size)]
    for block, (out_ref, i) in zip(blocks, places):
        x = block[...].astype(jnp.float32)
        scale = lax.rsqrt(jnp.mean(x * x, axis=-1, keepdims=True) + 1e-05)
        out_ref[pl.ds(i * rows, rows), :] = (x * scale * gain).astype(jnp.bfloat16)


def pack(groups, gain, after):
    blocks = sum(groups, [])
    sizes = tuple(len(group) for group in groups)
    rows, model = blocks[0].shape
    vmem = pl.BlockSpec(memory_space=pltpu.VMEM)
    return pl.pallas_call(
        functools.partial(pack_kernel, len(after), sizes),
        out_shape=tuple(jax.ShapeDtypeStruct((rows * size, model), jnp.bfloat16) for size in sizes),
        in_specs=[pl.BlockSpec(memory_space=pl.ANY)] * len(after) + [vmem] * (len(blocks) + 1),
        out_specs=(vmem,) * len(sizes),
        compiler_params=pltpu.CompilerParams(vmem_limit_bytes=8 * 2**20),
    )(*after, *blocks, gain)


def read_kernel(count, after, chip_ref, ids_hbm, weights_hbm, *refs):
    sources, (near_ref, far_ref, *refs) = refs[:count], refs[count + after :]
    targets, (ids_ref, weights_ref, sems) = refs[:count], refs[count:]
    pairs = [(ids_hbm, ids_ref), (weights_hbm, weights_ref), *zip(sources, targets)]
    copies = [pltpu.make_async_copy(a, b, sems.at[i]) for i, (a, b) in enumerate(pairs)]
    for copy in copies:
        copy.start()
    chosen, rows = ids_ref.shape
    half = near_ref.shape[1]
    expert = chip_ref[0] ^ lax.broadcasted_iota(jnp.int32, (2 * half, rows), 0)
    copies[0].wait()
    copies[1].wait()
    table = jnp.zeros((2 * half, rows), jnp.float32)
    for k in range(chosen):
        table += jnp.where(ids_ref[k : k + 1, :] == expert, weights_ref[k : k + 1, :], 0.0)
    near_ref[...] = table[:half].T
    far_ref[...] = table[half:].T
    for copy in copies[2:]:
        copy.wait()


def read(chip, expert_ids, expert_weights, half, arrays, after):
    rows, chosen = expert_ids.shape
    count = len(arrays)
    vmem, hbm = pl.BlockSpec(memory_space=pltpu.VMEM), pl.BlockSpec(memory_space=pltpu.HBM)
    table = jax.ShapeDtypeStruct((rows, half), jnp.float32)
    in_hbm = [pltpu.with_memory_space_constraint(a, pltpu.HBM) for a in (expert_ids.T, expert_weights.T, *arrays)]
    return pl.pallas_call(
        functools.partial(read_kernel, count, len(after)),
        out_shape=(table, table) + tuple(pltpu.VMEM(a.shape, a.dtype) for a in arrays),
        in_specs=[pl.BlockSpec(memory_space=pltpu.SMEM)]
        + [hbm] * len(in_hbm)
        + [pl.BlockSpec(memory_space=pl.ANY)] * len(after),
        out_specs=(vmem,) * (2 + count),
        scratch_shapes=[
            pltpu.VMEM((chosen, rows), expert_ids.dtype),
            pltpu.VMEM((chosen, rows), expert_weights.dtype),
            pltpu.SemaphoreType.DMA((2 + count,)),
        ],
        cost_estimate=pl.CostEstimate(
            flops=0, bytes_accessed=2 * sum(a.size * a.dtype.itemsize for a in arrays), transcendentals=0
        ),
        compiler_params=pltpu.CompilerParams(vmem_limit_bytes=16 * 2**20),
    )(chip, *in_hbm, *after)


def sum_kernel(masks, after, mine_ref, theirs_ref, *refs):
    for mask, out_ref in zip(masks, refs[after:]):
        rows = pl.ds(mask * out_ref.shape[0], out_ref.shape[0])
        total = mine_ref[rows, :].astype(jnp.float32) + theirs_ref[rows, :].astype(jnp.float32)
        out_ref[...] = total.astype(out_ref.dtype)


def sums(mine, theirs, rows, masks, after=()):
    vmem = pl.BlockSpec(memory_space=pltpu.VMEM)
    return pl.pallas_call(
        functools.partial(sum_kernel, masks, len(after)),
        out_shape=(jax.ShapeDtypeStruct((rows, mine.shape[1]), mine.dtype),) * len(masks),
        in_specs=[vmem] * 2 + [pl.BlockSpec(memory_space=pl.ANY)] * len(after),
        out_specs=(vmem,) * len(masks),
        compiler_params=pltpu.CompilerParams(vmem_limit_bytes=8 * 2**20),
    )(mine, theirs, *after)


def mix_kernel(table_ref, *refs):
    blocks, out_ref = refs[:-1], refs[-1]
    total = jnp.zeros(out_ref.shape, jnp.float32)
    for i, block in enumerate(blocks):
        total += table_ref[:, i : i + 1] * block[...].astype(jnp.float32)
    out_ref[...] = total.astype(out_ref.dtype)


def mixed(table, blocks):
    vmem = pl.BlockSpec(memory_space=pltpu.VMEM)
    return pl.pallas_call(
        mix_kernel,
        out_shape=jax.ShapeDtypeStruct(blocks[0].shape, blocks[0].dtype),
        in_specs=[vmem] * (len(blocks) + 1),
        out_specs=vmem,
        compiler_params=pltpu.CompilerParams(vmem_limit_bytes=8 * 2**20),
    )(table, *blocks)


def expert_kernel(count, *refs):
    groups, (gate_ref, up_ref, down_ref, table_ref) = refs[:count], refs[count : count + 4]
    outs, table_out_ref = refs[count + 4 : -1], refs[-1]
    table_out_ref[...] = table_ref[...]
    normed = jnp.concatenate([group[...] for group in groups])
    across = (((1,), (1,)), ((), ()))
    gate = lax.dot_general(normed, gate_ref[...], across, preferred_element_type=jnp.float32)
    upper = lax.dot_general(normed, up_ref[...], across, preferred_element_type=jnp.float32)
    act = (gate * jax.nn.sigmoid(1.702 * gate) * (upper + 1.0)).astype(jnp.bfloat16)
    out = jnp.dot(act, down_ref[...], preferred_element_type=jnp.float32).astype(jnp.bfloat16)
    start = 0
    for out_ref in outs:
        rows = out_ref.shape[0]
        out_ref[...] = out[start : start + rows]
        start += rows


def expert_parts(groups, sizes, gate_w, up_w, down_w, table):
    count, rows = len(groups), sum(sizes)
    hidden, model = gate_w.shape
    vmem = pl.BlockSpec(memory_space=pltpu.VMEM)
    return pl.pallas_call(
        functools.partial(expert_kernel, count),
        out_shape=tuple(jax.ShapeDtypeStruct((size, model), jnp.bfloat16) for size in sizes)
        + (jax.ShapeDtypeStruct(table.shape, table.dtype),),
        in_specs=[vmem] * (count + 4),
        out_specs=(vmem,) * (len(sizes) + 1),
        cost_estimate=pl.CostEstimate(
            flops=6 * rows * model * hidden, bytes_accessed=6 * model * hidden, transcendentals=rows * hidden
        ),
        compiler_params=pltpu.CompilerParams(vmem_limit_bytes=24 * 2**20),
    )(*groups, gate_w, up_w, down_w, table)


def halves(residual, norm_gain, expert_ids, expert_weights, gate_proj, up_proj, down_proj):
    rows, model = residual.shape
    chips = lax.axis_size("expert") // 2
    half = chips // 2

    def across(value, mask):
        pairs = [(i, i ^ (2 * mask)) for i in range(2 * chips)]
        return lax.ppermute(value, "expert", pairs) if mask else value

    def swap(value):
        return partner(value, "expert", 0)

    x = residual
    mirrored = across(x, half)
    near = [across(x, mask) for mask in range(1, half)]
    far = [across(mirrored, mask) for mask in range(1, half)]
    mirror_swapped = swap(mirrored)
    near_weights, far_weights, *held = read(
        (lax.axis_index("expert") // 2).reshape(1),
        expert_ids,
        expert_weights,
        half,
        (gate_proj[0].T, up_proj[0].T, down_proj[0]),
        (mirror_swapped, *near),
    )
    mine, mirror_theirs, mirror_mine = pack(
        (far + [x] + near, [mirror_swapped], [mirrored]), norm_gain, tuple(held)
    )
    *parts, far_weights = expert_parts(
        (mirror_theirs, swap(mine), mirror_mine, mine), (half * rows,) * 4, *held, far_weights
    )
    mirror_weights = across(far_weights, half)

    def give_back(mine, theirs, masks, after=()):
        done = sums(mine, theirs, rows, masks, after)
        return {mask: across(block, mask) for mask, block in zip(masks, done)}

    far_theirs, near_theirs, far_mine, near_mine = parts
    near_swapped = swap(near_theirs)
    far_blocks = give_back(far_mine, swap(far_theirs), tuple(range(half)))
    other = mixed(mirror_weights, [far_blocks[mask] for mask in range(half)])
    short = tuple(mask for mask in range(1, half) if mask & (mask - 1) == 0)
    long = tuple(mask for mask in range(half) if mask not in short)
    near_blocks = give_back(near_mine, near_swapped, long)
    near_blocks |= give_back(near_mine, near_swapped, short, (other,))
    total = x.astype(jnp.float32) + across(other, half).astype(jnp.float32)
    for mask, block in near_blocks.items():
        total += near_weights[:, mask][:, None] * block.astype(jnp.float32)
    return total.astype(jnp.bfloat16)


def body(residual, norm_gain, expert_ids, expert_weights, gate_proj, up_proj, down_proj):
    rows, chosen = expert_ids.shape
    chips = lax.axis_size("expert") // 2
    whole = 2 * rows * chosen // chips >= rows and chips >= 4 and chips & (chips - 1) == 0
    plan = halves if whole else slots
    return plan(residual, norm_gain, expert_ids, expert_weights, gate_proj, up_proj, down_proj)


def solution(mesh):
    in_specs = (
        P(("groups", "expert"), None),
        P(),
        P(("groups", "expert"), None),
        P(("groups", "expert"), None),
        P("expert", None, None),
        P("expert", None, None),
        P("expert", None, None),
    )
    out_specs = P(("groups", "expert"), None)
    return jax.shard_map(body, mesh=mesh, in_specs=in_specs, out_specs=out_specs, check_vma=False)
```

```python
import functools

import jax
import jax.numpy as jnp
from jax import lax
from jax.experimental import pallas as pl
from jax.experimental.pallas import tpu as pltpu
from jax.sharding import PartitionSpec as P


def partner(value, axis, bit):
    mask = 2**bit
    pairs = [(source, source ^ mask) for source in range(lax.axis_size(axis))]
    return lax.ppermute(value, axis, pairs)


def expert_half(flat, gate_w, up_w, down_w):
    gate = jnp.dot(flat, gate_w, preferred_element_type=jnp.float32)
    upper = jnp.dot(flat, up_w, preferred_element_type=jnp.float32)
    act = (gate * jax.nn.sigmoid(1.702 * gate) * (upper + 1.0)).astype(jnp.bfloat16)
    return jnp.dot(act, down_w, preferred_element_type=jnp.float32).astype(jnp.bfloat16)


def normalised(rows, norm_gain):
    x = rows.astype(jnp.float32)
    scale = lax.rsqrt(jnp.mean(x * x, axis=-1, keepdims=True) + 1e-05)
    return (x * scale * norm_gain).astype(jnp.bfloat16)


def pair_sum(mine, theirs):
    return (mine.astype(jnp.float32) + theirs.astype(jnp.float32)).astype(jnp.bfloat16)


def slots(residual, norm_gain, expert_ids, expert_weights, gate_proj, up_proj, down_proj):
    rows, model = residual.shape
    chosen = expert_ids.shape[1]
    devices = lax.axis_size("expert")
    experts = devices // 2
    capacity = 2 * rows * chosen // experts
    half_cap = capacity // 2
    gate_w, up_w, down_w = (gate_proj[0], up_proj[0], down_proj[0])
    normed = normalised(residual, norm_gain)
    flat_ids = expert_ids.reshape(rows * chosen)
    onehot = (
        flat_ids[:, None] == lax.broadcasted_iota(jnp.int32, (rows * chosen, experts), 1)
    ).astype(jnp.int32)
    slot = jnp.sum(onehot * jnp.cumsum(onehot, axis=0), axis=1) - 1
    position = flat_ids * capacity + slot
    pick = (
        position[:, None] == lax.broadcasted_iota(jnp.int32, (rows * chosen, experts * capacity), 1)
    ).astype(jnp.float32)
    place_rows = jnp.sum(pick.reshape(rows, chosen, experts * capacity), axis=1)
    send = lax.dot_general(
        place_rows.astype(jnp.bfloat16),
        normed,
        (((0,), (0,)), ((), ())),
        preferred_element_type=jnp.float32,
    )
    outgoing = send.astype(jnp.bfloat16).reshape(devices, half_cap, model)
    arrived = lax.all_to_all(outgoing, "expert", split_axis=0, concat_axis=0, tiled=True)
    other = partner(arrived, "expert", 0)
    both = jnp.stack((arrived, other)).reshape(2 * devices * half_cap, model)
    both = expert_half(both, gate_w, up_w, down_w).reshape(2, devices, half_cap, model)
    returned = partner(both[1], "expert", 0)
    finished = pair_sum(both[0], returned)
    back = lax.all_to_all(finished, "expert", split_axis=0, concat_axis=0, tiled=True)
    weighted = jnp.sum(
        (pick * expert_weights.reshape(rows * chosen)[:, None]).reshape(
            rows, chosen, experts * capacity
        ),
        axis=1,
    )
    combined = jnp.dot(
        weighted,
        back.reshape(experts * capacity, model).astype(jnp.float32),
        precision=lax.Precision.HIGHEST,
    )
    return (residual.astype(jnp.float32) + combined).astype(jnp.bfloat16)


def pack_kernel(after, sizes, *refs):
    blocks, gain_ref, outs = refs[after : -1 - len(sizes)], refs[-1 - len(sizes)], refs[-len(sizes) :]
    rows, model = blocks[0].shape
    gain = gain_ref[...].reshape(1, model)
    places = [(out, i) for out, size in zip(outs, sizes) for i in range(size)]
    for block, (out_ref, i) in zip(blocks, places):
        x = block[...].astype(jnp.float32)
        scale = lax.rsqrt(jnp.mean(x * x, axis=-1, keepdims=True) + 1e-05)
        out_ref[pl.ds(i * rows, rows), :] = (x * scale * gain).astype(jnp.bfloat16)


def pack(groups, gain, after):
    blocks = sum(groups, [])
    sizes = tuple(len(group) for group in groups)
    rows, model = blocks[0].shape
    vmem = pl.BlockSpec(memory_space=pltpu.VMEM)
    return pl.pallas_call(
        functools.partial(pack_kernel, len(after), sizes),
        out_shape=tuple(jax.ShapeDtypeStruct((rows * size, model), jnp.bfloat16) for size in sizes),
        in_specs=[pl.BlockSpec(memory_space=pl.ANY)] * len(after) + [vmem] * (len(blocks) + 1),
        out_specs=(vmem,) * len(sizes),
        compiler_params=pltpu.CompilerParams(vmem_limit_bytes=8 * 2**20),
    )(*after, *blocks, gain)


def relay_kernel(after, *refs):
    block_ref, own_ref, gain_ref, out_ref, both_ref = refs[after:]
    rows, model = block_ref.shape
    gain = gain_ref[...].reshape(1, model)
    for i, ref in enumerate((block_ref, own_ref)):
        x = ref[...].astype(jnp.float32)
        scale = lax.rsqrt(jnp.mean(x * x, axis=-1, keepdims=True) + 1e-05)
        normed = (x * scale * gain).astype(jnp.bfloat16)
        both_ref[pl.ds(i * rows, rows), :] = normed
        if i == 0:
            out_ref[...] = normed


def relay(block, own, gain, after):
    rows, model = block.shape
    vmem = pl.BlockSpec(memory_space=pltpu.VMEM)
    return pl.pallas_call(
        functools.partial(relay_kernel, len(after)),
        out_shape=tuple(jax.ShapeDtypeStruct((n * rows, model), jnp.bfloat16) for n in (1, 2)),
        in_specs=[pl.BlockSpec(memory_space=pl.ANY)] * len(after) + [vmem] * 3,
        out_specs=(vmem,) * 2,
        compiler_params=pltpu.CompilerParams(vmem_limit_bytes=8 * 2**20),
    )(*after, block, own, gain)


def mix_kernel(table_ref, *refs):
    blocks, out_ref = refs[:-1], refs[-1]
    total = jnp.zeros(out_ref.shape, jnp.float32)
    for i, block in enumerate(blocks):
        total += table_ref[:, i : i + 1] * block[...].astype(jnp.float32)
    out_ref[...] = total.astype(out_ref.dtype)


def mixed(table, blocks):
    vmem = pl.BlockSpec(memory_space=pltpu.VMEM)
    return pl.pallas_call(
        mix_kernel,
        out_shape=jax.ShapeDtypeStruct(blocks[0].shape, blocks[0].dtype),
        in_specs=[vmem] * (len(blocks) + 1),
        out_specs=vmem,
        compiler_params=pltpu.CompilerParams(vmem_limit_bytes=8 * 2**20),
    )(table, *blocks)


def expert_kernel(count, pieces, rows, *refs):
    arrays, (gate_ref, up_ref, down_ref, table_ref) = refs[:count], refs[count : count + 4]
    outs, table_out_ref = refs[count + 4 : -1], refs[-1]
    table_out_ref[...] = table_ref[...]
    normed = jnp.concatenate([arrays[i][block * rows : (block + 1) * rows, :] for i, block in pieces])
    across = (((1,), (1,)), ((), ()))
    gate = lax.dot_general(normed, gate_ref[...], across, preferred_element_type=jnp.float32)
    upper = lax.dot_general(normed, up_ref[...], across, preferred_element_type=jnp.float32)
    act = (gate * jax.nn.sigmoid(1.702 * gate) * (upper + 1.0)).astype(jnp.bfloat16)
    out = jnp.dot(act, down_ref[...], preferred_element_type=jnp.float32).astype(jnp.bfloat16)
    start = 0
    for out_ref in outs:
        rows = out_ref.shape[0]
        out_ref[...] = out[start : start + rows]
        start += rows


def expert_parts(groups, rows, gate_w, up_w, down_w, table):
    arrays = []
    pieces = []
    for array, block in sum(groups, []):
        known = [i for i, other in enumerate(arrays) if other is array]
        pieces.append((known[0] if known else len(arrays), block))
        arrays += [] if known else [array]
    sizes = tuple(rows * len(group) for group in groups)
    count = len(arrays)
    hidden, model = gate_w.shape
    vmem = pl.BlockSpec(memory_space=pltpu.VMEM)
    return pl.pallas_call(
        functools.partial(expert_kernel, count, tuple(pieces), rows),
        out_shape=tuple(jax.ShapeDtypeStruct((size, model), jnp.bfloat16) for size in sizes)
        + (jax.ShapeDtypeStruct(table.shape, table.dtype),),
        in_specs=[vmem] * (count + 4),
        out_specs=(vmem,) * (len(sizes) + 1),
        cost_estimate=pl.CostEstimate(
            flops=6 * sum(sizes) * model * hidden,
            bytes_accessed=6 * model * hidden,
            transcendentals=sum(sizes) * hidden,
        ),
        compiler_params=pltpu.CompilerParams(vmem_limit_bytes=24 * 2**20),
    )(*arrays, gate_w, up_w, down_w, table)


def read_kernel(after, *refs):
    refs, sems = refs[after:-1], refs[-1]
    sources, targets = refs[: len(refs) // 2], refs[len(refs) // 2 :]
    copies = [
        pltpu.make_async_copy(source, target, sems.at[i])
        for i, (source, target) in enumerate(zip(sources, targets))
    ]
    for copy in copies:
        copy.start()
    for copy in copies:
        copy.wait()


def read(arrays, after):
    count = len(arrays)
    vmem, hbm = pl.BlockSpec(memory_space=pltpu.VMEM), pl.BlockSpec(memory_space=pltpu.HBM)
    return pl.pallas_call(
        functools.partial(read_kernel, len(after)),
        out_shape=tuple(pltpu.VMEM(a.shape, a.dtype) for a in arrays),
        in_specs=[pl.BlockSpec(memory_space=pl.ANY)] * len(after) + [hbm] * count,
        out_specs=(vmem,) * count,
        scratch_shapes=[pltpu.SemaphoreType.DMA((count,))],
        cost_estimate=pl.CostEstimate(
            flops=0, bytes_accessed=2 * sum(a.size * a.dtype.itemsize for a in arrays), transcendentals=0
        ),
        compiler_params=pltpu.CompilerParams(vmem_limit_bytes=16 * 2**20),
    )(*after, *(pltpu.with_memory_space_constraint(a, pltpu.HBM) for a in arrays))


def load_kernel(chip_ref, ids_hbm, weights_hbm, source, near_ref, far_ref, target, ids_ref, weights_ref, sems):
    copies = [
        pltpu.make_async_copy(a, b, sems.at[i])
        for i, (a, b) in enumerate(((ids_hbm, ids_ref), (weights_hbm, weights_ref), (source, target)))
    ]
    for copy in copies:
        copy.start()
    chosen, rows = ids_ref.shape
    half = near_ref.shape[1]
    expert = chip_ref[0] ^ lax.broadcasted_iota(jnp.int32, (2 * half, rows), 0)
    copies[0].wait()
    copies[1].wait()
    table = jnp.zeros((2 * half, rows), jnp.float32)
    for k in range(chosen):
        table += jnp.where(ids_ref[k : k + 1, :] == expert, weights_ref[k : k + 1, :], 0.0)
    near_ref[...] = table[:half].T
    far_ref[...] = table[half:].T
    copies[2].wait()


def load(chip, expert_ids, expert_weights, half, array):
    rows, chosen = expert_ids.shape
    vmem, hbm = pl.BlockSpec(memory_space=pltpu.VMEM), pl.BlockSpec(memory_space=pltpu.HBM)
    table = jax.ShapeDtypeStruct((rows, half), jnp.float32)
    return pl.pallas_call(
        load_kernel,
        out_shape=(table, table, pltpu.VMEM(array.shape, array.dtype)),
        in_specs=[pl.BlockSpec(memory_space=pltpu.SMEM), hbm, hbm, hbm],
        out_specs=(vmem,) * 3,
        scratch_shapes=[
            pltpu.VMEM((chosen, rows), expert_ids.dtype),
            pltpu.VMEM((chosen, rows), expert_weights.dtype),
            pltpu.SemaphoreType.DMA((3,)),
        ],
        cost_estimate=pl.CostEstimate(
            flops=0, bytes_accessed=2 * array.size * array.dtype.itemsize, transcendentals=0
        ),
        compiler_params=pltpu.CompilerParams(vmem_limit_bytes=16 * 2**20),
    )(
        chip,
        *(pltpu.with_memory_space_constraint(a, pltpu.HBM) for a in (expert_ids.T, expert_weights.T, array)),
    )


def halves(residual, norm_gain, expert_ids, expert_weights, gate_proj, up_proj, down_proj):
    rows, model = residual.shape
    chips = lax.axis_size("expert") // 2
    half = chips // 2

    def across(value, mask):
        pairs = [(i, i ^ (2 * mask)) for i in range(2 * chips)]
        return lax.ppermute(value, "expert", pairs) if mask else value

    def swap(value):
        return partner(value, "expert", 0)

    x = residual
    mirrored = across(x, half)
    short = [mask for mask in range(1, half) if mask & (mask - 1) == 0]
    long = [mask for mask in range(1, half) if mask not in short]
    near = [across(x, mask) for mask in short]
    chip = (lax.axis_index("expert") // 2).reshape(1)
    near_weights, far_weights, gate_w = load(chip, expert_ids, expert_weights, half, gate_proj[0].T)
    mirrored, both = relay(mirrored, x, norm_gain, (near_weights, *near))
    far = {0: mirrored} | {mask: across(mirrored, mask) for mask in short} | {mask: across(both, mask) for mask in long}
    far_swapped = {0: swap(mirrored)}
    up_w, down_w = read((up_proj[0].T, down_proj[0]), (far_swapped[0], *near))
    far_swapped |= {mask: swap(far[mask]) for mask in short + long}
    (near_rows,) = pack(([x] + near,), norm_gain, (up_w, *(far[mask] for mask in short + long)))

    def groups(far, near):
        at = {mask: (near, i) for i, mask in enumerate([0] + short)} | {mask: (far[mask], 1) for mask in long}
        return [(far[mask], 0) for mask in range(half)], [at[mask] for mask in range(half)]

    far_theirs, near_theirs = groups(far_swapped, swap(near_rows))
    far_mine, near_mine = groups(far, near_rows)
    *parts, far_weights = expert_parts(
        (far_theirs, far_mine, near_theirs, near_mine), rows, gate_w, up_w, down_w, far_weights
    )
    mirror_weights = across(far_weights, half)

    def give_back(done):
        done = done.reshape(half, rows, model)
        return [across(done[mask], mask) for mask in range(half)]

    far_blocks = give_back(pair_sum(parts[1], swap(parts[0])))
    near_blocks = give_back(pair_sum(parts[3], swap(parts[2])))
    total = x.astype(jnp.float32) + across(mixed(mirror_weights, far_blocks), half).astype(jnp.float32)
    for mask, block in enumerate(near_blocks):
        total += near_weights[:, mask][:, None] * block.astype(jnp.float32)
    return total.astype(jnp.bfloat16)


def body(residual, norm_gain, expert_ids, expert_weights, gate_proj, up_proj, down_proj):
    rows, chosen = expert_ids.shape
    chips = lax.axis_size("expert") // 2
    whole = 2 * rows * chosen // chips >= rows and chips >= 4 and chips & (chips - 1) == 0
    plan = halves if whole else slots
    return plan(residual, norm_gain, expert_ids, expert_weights, gate_proj, up_proj, down_proj)


def solution(mesh):
    in_specs = (
        P(("groups", "expert"), None),
        P(),
        P(("groups", "expert"), None),
        P(("groups", "expert"), None),
        P("expert", None, None),
        P("expert", None, None),
        P("expert", None, None),
    )
    out_specs = P(("groups", "expert"), None)
    return jax.shard_map(body, mesh=mesh, in_specs=in_specs, out_specs=out_specs, check_vma=False)
```

```python
import functools

import jax
import jax.numpy as jnp
from jax import lax
from jax.experimental import pallas as pl
from jax.experimental.pallas import tpu as pltpu
from jax.sharding import PartitionSpec as P


def partner(value, axis, bit):
    mask = 2**bit
    pairs = [(source, source ^ mask) for source in range(lax.axis_size(axis))]
    return lax.ppermute(value, axis, pairs)


def expert_half(flat, gate_w, up_w, down_w):
    gate = jnp.dot(flat, gate_w, preferred_element_type=jnp.float32)
    upper = jnp.dot(flat, up_w, preferred_element_type=jnp.float32)
    act = (gate * jax.nn.sigmoid(1.702 * gate) * (upper + 1.0)).astype(jnp.bfloat16)
    return jnp.dot(act, down_w, preferred_element_type=jnp.float32).astype(jnp.bfloat16)


def normalised(rows, norm_gain):
    x = rows.astype(jnp.float32)
    scale = lax.rsqrt(jnp.mean(x * x, axis=-1, keepdims=True) + 1e-05)
    return (x * scale * norm_gain).astype(jnp.bfloat16)


def pair_sum(mine, theirs):
    return (mine.astype(jnp.float32) + theirs.astype(jnp.float32)).astype(jnp.bfloat16)


def slots(residual, norm_gain, expert_ids, expert_weights, gate_proj, up_proj, down_proj):
    rows, model = residual.shape
    chosen = expert_ids.shape[1]
    devices = lax.axis_size("expert")
    experts = devices // 2
    capacity = 2 * rows * chosen // experts
    half_cap = capacity // 2
    gate_w, up_w, down_w = (gate_proj[0], up_proj[0], down_proj[0])
    normed = normalised(residual, norm_gain)
    flat_ids = expert_ids.reshape(rows * chosen)
    onehot = (
        flat_ids[:, None] == lax.broadcasted_iota(jnp.int32, (rows * chosen, experts), 1)
    ).astype(jnp.int32)
    slot = jnp.sum(onehot * jnp.cumsum(onehot, axis=0), axis=1) - 1
    position = flat_ids * capacity + slot
    pick = (
        position[:, None] == lax.broadcasted_iota(jnp.int32, (rows * chosen, experts * capacity), 1)
    ).astype(jnp.float32)
    place_rows = jnp.sum(pick.reshape(rows, chosen, experts * capacity), axis=1)
    send = lax.dot_general(
        place_rows.astype(jnp.bfloat16),
        normed,
        (((0,), (0,)), ((), ())),
        preferred_element_type=jnp.float32,
    )
    outgoing = send.astype(jnp.bfloat16).reshape(devices, half_cap, model)
    arrived = lax.all_to_all(outgoing, "expert", split_axis=0, concat_axis=0, tiled=True)
    other = partner(arrived, "expert", 0)
    both = jnp.stack((arrived, other)).reshape(2 * devices * half_cap, model)
    both = expert_half(both, gate_w, up_w, down_w).reshape(2, devices, half_cap, model)
    returned = partner(both[1], "expert", 0)
    finished = pair_sum(both[0], returned)
    back = lax.all_to_all(finished, "expert", split_axis=0, concat_axis=0, tiled=True)
    weighted = jnp.sum(
        (pick * expert_weights.reshape(rows * chosen)[:, None]).reshape(
            rows, chosen, experts * capacity
        ),
        axis=1,
    )
    combined = jnp.dot(
        weighted,
        back.reshape(experts * capacity, model).astype(jnp.float32),
        precision=lax.Precision.HIGHEST,
    )
    return (residual.astype(jnp.float32) + combined).astype(jnp.bfloat16)


def pack_kernel(after, sizes, *refs):
    blocks, gain_ref, outs = refs[after : -1 - len(sizes)], refs[-1 - len(sizes)], refs[-len(sizes) :]
    rows, model = blocks[0].shape
    gain = gain_ref[...].reshape(1, model)
    places = [(out, i) for out, size in zip(outs, sizes) for i in range(size)]
    for block, (out_ref, i) in zip(blocks, places):
        x = block[...].astype(jnp.float32)
        scale = lax.rsqrt(jnp.mean(x * x, axis=-1, keepdims=True) + 1e-05)
        out_ref[pl.ds(i * rows, rows), :] = (x * scale * gain).astype(jnp.bfloat16)


def pack(groups, gain, after):
    blocks = sum(groups, [])
    sizes = tuple(len(group) for group in groups)
    rows, model = blocks[0].shape
    vmem = pl.BlockSpec(memory_space=pltpu.VMEM)
    return pl.pallas_call(
        functools.partial(pack_kernel, len(after), sizes),
        out_shape=tuple(jax.ShapeDtypeStruct((rows * size, model), jnp.bfloat16) for size in sizes),
        in_specs=[pl.BlockSpec(memory_space=pl.ANY)] * len(after) + [vmem] * (len(blocks) + 1),
        out_specs=(vmem,) * len(sizes),
        compiler_params=pltpu.CompilerParams(vmem_limit_bytes=8 * 2**20),
    )(*after, *blocks, gain)


def mix_kernel(columns, table_ref, *refs):
    blocks, out_ref = refs[:-1], refs[-1]
    total = jnp.zeros(out_ref.shape, jnp.float32)
    for column, block in zip(columns, blocks):
        total += table_ref[:, column : column + 1] * block[...].astype(jnp.float32)
    out_ref[...] = total.astype(out_ref.dtype)


def mixed(table, columns, blocks):
    vmem = pl.BlockSpec(memory_space=pltpu.VMEM)
    return pl.pallas_call(
        functools.partial(mix_kernel, columns),
        out_shape=jax.ShapeDtypeStruct(blocks[0].shape, blocks[0].dtype),
        in_specs=[vmem] * (len(blocks) + 1),
        out_specs=vmem,
        compiler_params=pltpu.CompilerParams(vmem_limit_bytes=8 * 2**20),
    )(table, *blocks)


def expert_kernel(count, *refs):
    groups, (gate_ref, up_ref, down_ref, table_ref) = refs[:count], refs[count : count + 4]
    outs, table_out_ref = refs[count + 4 : -1], refs[-1]
    table_out_ref[...] = table_ref[...]
    normed = jnp.concatenate([group[...] for group in groups])
    across = (((1,), (1,)), ((), ()))
    gate = lax.dot_general(normed, gate_ref[...], across, preferred_element_type=jnp.float32)
    upper = lax.dot_general(normed, up_ref[...], across, preferred_element_type=jnp.float32)
    act = (gate * jax.nn.sigmoid(1.702 * gate) * (upper + 1.0)).astype(jnp.bfloat16)
    out = jnp.dot(act, down_ref[...], preferred_element_type=jnp.float32).astype(jnp.bfloat16)
    start = 0
    for out_ref in outs:
        rows = out_ref.shape[0]
        out_ref[...] = out[start : start + rows]
        start += rows


def expert_parts(groups, sizes, gate_w, up_w, down_w, table):
    count, rows = len(groups), sum(sizes)
    hidden, model = gate_w.shape
    vmem = pl.BlockSpec(memory_space=pltpu.VMEM)
    return pl.pallas_call(
        functools.partial(expert_kernel, count),
        out_shape=tuple(jax.ShapeDtypeStruct((size, model), jnp.bfloat16) for size in sizes)
        + (jax.ShapeDtypeStruct(table.shape, table.dtype),),
        in_specs=[vmem] * (count + 4),
        out_specs=(vmem,) * (len(sizes) + 1),
        cost_estimate=pl.CostEstimate(
            flops=6 * rows * model * hidden, bytes_accessed=6 * model * hidden, transcendentals=rows * hidden
        ),
        compiler_params=pltpu.CompilerParams(vmem_limit_bytes=24 * 2**20),
    )(*groups, gate_w, up_w, down_w, table)


def read_kernel(after, *refs):
    refs, sems = refs[after:-1], refs[-1]
    sources, targets = refs[: len(refs) // 2], refs[len(refs) // 2 :]
    copies = [
        pltpu.make_async_copy(source, target, sems.at[i])
        for i, (source, target) in enumerate(zip(sources, targets))
    ]
    for copy in copies:
        copy.start()
    for copy in copies:
        copy.wait()


def read(arrays, after):
    count = len(arrays)
    vmem, hbm = pl.BlockSpec(memory_space=pltpu.VMEM), pl.BlockSpec(memory_space=pltpu.HBM)
    return pl.pallas_call(
        functools.partial(read_kernel, len(after)),
        out_shape=tuple(pltpu.VMEM(a.shape, a.dtype) for a in arrays),
        in_specs=[pl.BlockSpec(memory_space=pl.ANY)] * len(after) + [hbm] * count,
        out_specs=(vmem,) * count,
        scratch_shapes=[pltpu.SemaphoreType.DMA((count,))],
        cost_estimate=pl.CostEstimate(
            flops=0, bytes_accessed=2 * sum(a.size * a.dtype.itemsize for a in arrays), transcendentals=0
        ),
        compiler_params=pltpu.CompilerParams(vmem_limit_bytes=16 * 2**20),
    )(*after, *(pltpu.with_memory_space_constraint(a, pltpu.HBM) for a in arrays))


def load_kernel(chip_ref, ids_hbm, weights_hbm, source, near_ref, far_ref, target, ids_ref, weights_ref, sems):
    copies = [
        pltpu.make_async_copy(a, b, sems.at[i])
        for i, (a, b) in enumerate(((ids_hbm, ids_ref), (weights_hbm, weights_ref), (source, target)))
    ]
    for copy in copies:
        copy.start()
    chosen, rows = ids_ref.shape
    half = near_ref.shape[1]
    expert = chip_ref[0] ^ lax.broadcasted_iota(jnp.int32, (2 * half, rows), 0)
    copies[0].wait()
    copies[1].wait()
    table = jnp.zeros((2 * half, rows), jnp.float32)
    for k in range(chosen):
        table += jnp.where(ids_ref[k : k + 1, :] == expert, weights_ref[k : k + 1, :], 0.0)
    near_ref[...] = table[:half].T
    far_ref[...] = table[half:].T
    copies[2].wait()


def load(chip, expert_ids, expert_weights, half, array):
    rows, chosen = expert_ids.shape
    vmem, hbm = pl.BlockSpec(memory_space=pltpu.VMEM), pl.BlockSpec(memory_space=pltpu.HBM)
    table = jax.ShapeDtypeStruct((rows, half), jnp.float32)
    return pl.pallas_call(
        load_kernel,
        out_shape=(table, table, pltpu.VMEM(array.shape, array.dtype)),
        in_specs=[pl.BlockSpec(memory_space=pltpu.SMEM), hbm, hbm, hbm],
        out_specs=(vmem,) * 3,
        scratch_shapes=[
            pltpu.VMEM((chosen, rows), expert_ids.dtype),
            pltpu.VMEM((chosen, rows), expert_weights.dtype),
            pltpu.SemaphoreType.DMA((3,)),
        ],
        cost_estimate=pl.CostEstimate(
            flops=0, bytes_accessed=2 * array.size * array.dtype.itemsize, transcendentals=0
        ),
        compiler_params=pltpu.CompilerParams(vmem_limit_bytes=16 * 2**20),
    )(
        chip,
        *(pltpu.with_memory_space_constraint(a, pltpu.HBM) for a in (expert_ids.T, expert_weights.T, array)),
    )


def halves(residual, norm_gain, expert_ids, expert_weights, gate_proj, up_proj, down_proj):
    rows, model = residual.shape
    chips = lax.axis_size("expert") // 2
    half = chips // 2

    def across(value, mask):
        pairs = [(i, i ^ (2 * mask)) for i in range(2 * chips)]
        return lax.ppermute(value, "expert", pairs) if mask else value

    def swap(value):
        return partner(value, "expert", 0)

    x = residual
    mirrored = across(x, half)
    near = [across(x, mask) for mask in range(1, half)]
    chip = (lax.axis_index("expert") // 2).reshape(1)
    near_weights, far_weights, gate_w = load(chip, expert_ids, expert_weights, half, gate_proj[0].T)
    (mirrored,) = pack(([mirrored],), norm_gain, (near_weights,))
    far = [across(mirrored, mask) for mask in range(1, half)]
    mirror_swapped = swap(mirrored)
    up_w, down_w = read((up_proj[0].T, down_proj[0]), (mirror_swapped, *near))
    far_swapped = [swap(block) for block in far]
    (near_rows,) = pack(([x] + near,), norm_gain, (up_w, *far))
    *parts, far_weights = expert_parts(
        (mirror_swapped, *far_swapped, mirrored, *far, swap(near_rows), near_rows),
        (half * rows,) * 4,
        gate_w,
        up_w,
        down_w,
        far_weights,
    )
    mirror_weights = across(far_weights, half)

    def blocks_of(done):
        return list(done.reshape(half, rows, model))

    done = blocks_of(pair_sum(parts[1], swap(parts[0])))
    via = (0,) + tuple(mask for mask in range(1, half) if mask & (mask - 1) == 0)
    other = mixed(mirror_weights, via, [across(done[mask], mask) for mask in via])
    home = [
        (far_weights[:, mask], across(done[mask], half ^ mask)) for mask in range(half) if mask not in via
    ]
    done = blocks_of(pair_sum(parts[3], swap(parts[2])))
    home += [(near_weights[:, mask], across(done[mask], mask)) for mask in range(half)]
    total = x.astype(jnp.float32) + across(other, half).astype(jnp.float32)
    for column, block in home:
        total += column[:, None] * block.astype(jnp.float32)
    return total.astype(jnp.bfloat16)


def body(residual, norm_gain, expert_ids, expert_weights, gate_proj, up_proj, down_proj):
    rows, chosen = expert_ids.shape
    chips = lax.axis_size("expert") // 2
    whole = 2 * rows * chosen // chips >= rows and chips >= 4 and chips & (chips - 1) == 0
    plan = halves if whole else slots
    return plan(residual, norm_gain, expert_ids, expert_weights, gate_proj, up_proj, down_proj)


def solution(mesh):
    in_specs = (
        P(("groups", "expert"), None),
        P(),
        P(("groups", "expert"), None),
        P(("groups", "expert"), None),
        P("expert", None, None),
        P("expert", None, None),
        P("expert", None, None),
    )
    out_specs = P(("groups", "expert"), None)
    return jax.shard_map(body, mesh=mesh, in_specs=in_specs, out_specs=out_specs, check_vma=False)
```

```python
import functools

import jax
import jax.numpy as jnp
from jax import lax
from jax.experimental import pallas as pl
from jax.experimental.pallas import tpu as pltpu
from jax.sharding import PartitionSpec as P


def partner(value, axis, bit):
    mask = 2**bit
    pairs = [(source, source ^ mask) for source in range(lax.axis_size(axis))]
    return lax.ppermute(value, axis, pairs)


def expert_half(flat, gate_w, up_w, down_w):
    gate = jnp.dot(flat, gate_w, preferred_element_type=jnp.float32)
    upper = jnp.dot(flat, up_w, preferred_element_type=jnp.float32)
    act = (gate * jax.nn.sigmoid(1.702 * gate) * (upper + 1.0)).astype(jnp.bfloat16)
    return jnp.dot(act, down_w, preferred_element_type=jnp.float32).astype(jnp.bfloat16)


def normalised(rows, norm_gain):
    x = rows.astype(jnp.float32)
    scale = lax.rsqrt(jnp.mean(x * x, axis=-1, keepdims=True) + 1e-05)
    return (x * scale * norm_gain).astype(jnp.bfloat16)


def pair_sum(mine, theirs):
    return (mine.astype(jnp.float32) + theirs.astype(jnp.float32)).astype(jnp.bfloat16)


def slots(residual, norm_gain, expert_ids, expert_weights, gate_proj, up_proj, down_proj):
    rows, model = residual.shape
    chosen = expert_ids.shape[1]
    devices = lax.axis_size("expert")
    experts = devices // 2
    capacity = 2 * rows * chosen // experts
    half_cap = capacity // 2
    gate_w, up_w, down_w = (gate_proj[0], up_proj[0], down_proj[0])
    normed = normalised(residual, norm_gain)
    flat_ids = expert_ids.reshape(rows * chosen)
    onehot = (
        flat_ids[:, None] == lax.broadcasted_iota(jnp.int32, (rows * chosen, experts), 1)
    ).astype(jnp.int32)
    slot = jnp.sum(onehot * jnp.cumsum(onehot, axis=0), axis=1) - 1
    position = flat_ids * capacity + slot
    pick = (
        position[:, None] == lax.broadcasted_iota(jnp.int32, (rows * chosen, experts * capacity), 1)
    ).astype(jnp.float32)
    place_rows = jnp.sum(pick.reshape(rows, chosen, experts * capacity), axis=1)
    send = lax.dot_general(
        place_rows.astype(jnp.bfloat16),
        normed,
        (((0,), (0,)), ((), ())),
        preferred_element_type=jnp.float32,
    )
    outgoing = send.astype(jnp.bfloat16).reshape(devices, half_cap, model)
    arrived = lax.all_to_all(outgoing, "expert", split_axis=0, concat_axis=0, tiled=True)
    other = partner(arrived, "expert", 0)
    both = jnp.stack((arrived, other)).reshape(2 * devices * half_cap, model)
    both = expert_half(both, gate_w, up_w, down_w).reshape(2, devices, half_cap, model)
    returned = partner(both[1], "expert", 0)
    finished = pair_sum(both[0], returned)
    back = lax.all_to_all(finished, "expert", split_axis=0, concat_axis=0, tiled=True)
    weighted = jnp.sum(
        (pick * expert_weights.reshape(rows * chosen)[:, None]).reshape(
            rows, chosen, experts * capacity
        ),
        axis=1,
    )
    combined = jnp.dot(
        weighted,
        back.reshape(experts * capacity, model).astype(jnp.float32),
        precision=lax.Precision.HIGHEST,
    )
    return (residual.astype(jnp.float32) + combined).astype(jnp.bfloat16)


def pack_kernel(after, sizes, *refs):
    blocks, gain_ref, outs = refs[after : -1 - len(sizes)], refs[-1 - len(sizes)], refs[-len(sizes) :]
    rows, model = blocks[0].shape
    gain = gain_ref[...].reshape(1, model)
    places = [(out, i) for out, size in zip(outs, sizes) for i in range(size)]
    for block, (out_ref, i) in zip(blocks, places):
        x = block[...].astype(jnp.float32)
        scale = lax.rsqrt(jnp.mean(x * x, axis=-1, keepdims=True) + 1e-05)
        out_ref[pl.ds(i * rows, rows), :] = (x * scale * gain).astype(jnp.bfloat16)


def pack(groups, gain, after):
    blocks = sum(groups, [])
    sizes = tuple(len(group) for group in groups)
    rows, model = blocks[0].shape
    vmem = pl.BlockSpec(memory_space=pltpu.VMEM)
    return pl.pallas_call(
        functools.partial(pack_kernel, len(after), sizes),
        out_shape=tuple(jax.ShapeDtypeStruct((rows * size, model), jnp.bfloat16) for size in sizes),
        in_specs=[pl.BlockSpec(memory_space=pl.ANY)] * len(after) + [vmem] * (len(blocks) + 1),
        out_specs=(vmem,) * len(sizes),
        compiler_params=pltpu.CompilerParams(vmem_limit_bytes=8 * 2**20),
    )(*after, *blocks, gain)


def mix_kernel(table_ref, *refs):
    blocks, out_ref = refs[:-1], refs[-1]
    total = jnp.zeros(out_ref.shape, jnp.float32)
    for i, block in enumerate(blocks):
        total += table_ref[:, i : i + 1] * block[...].astype(jnp.float32)
    out_ref[...] = total.astype(out_ref.dtype)


def mixed(table, blocks):
    vmem = pl.BlockSpec(memory_space=pltpu.VMEM)
    return pl.pallas_call(
        mix_kernel,
        out_shape=jax.ShapeDtypeStruct(blocks[0].shape, blocks[0].dtype),
        in_specs=[vmem] * (len(blocks) + 1),
        out_specs=vmem,
        compiler_params=pltpu.CompilerParams(vmem_limit_bytes=8 * 2**20),
    )(table, *blocks)


def expert_kernel(count, *refs):
    groups, (gate_ref, up_ref, down_ref, table_ref) = refs[:count], refs[count : count + 4]
    outs, table_out_ref = refs[count + 4 : -1], refs[-1]
    table_out_ref[...] = table_ref[...]
    normed = jnp.concatenate([group[...] for group in groups])
    across = (((1,), (1,)), ((), ()))
    gate = lax.dot_general(gate_ref[...], normed, across, preferred_element_type=jnp.float32)
    upper = lax.dot_general(up_ref[...], normed, across, preferred_element_type=jnp.float32)
    act = (gate * jax.nn.sigmoid(1.702 * gate) * (upper + 1.0)).astype(jnp.bfloat16).T
    out = jnp.dot(act, down_ref[...], preferred_element_type=jnp.float32).astype(jnp.bfloat16)
    start = 0
    for out_ref in outs:
        rows = out_ref.shape[0]
        out_ref[...] = out[start : start + rows]
        start += rows


def expert_parts(groups, sizes, gate_w, up_w, down_w, table):
    count, rows = len(groups), sum(sizes)
    hidden, model = gate_w.shape
    vmem = pl.BlockSpec(memory_space=pltpu.VMEM)
    return pl.pallas_call(
        functools.partial(expert_kernel, count),
        out_shape=tuple(jax.ShapeDtypeStruct((size, model), jnp.bfloat16) for size in sizes)
        + (jax.ShapeDtypeStruct(table.shape, table.dtype),),
        in_specs=[vmem] * (count + 4),
        out_specs=(vmem,) * (len(sizes) + 1),
        cost_estimate=pl.CostEstimate(
            flops=6 * rows * model * hidden, bytes_accessed=6 * model * hidden, transcendentals=rows * hidden
        ),
        compiler_params=pltpu.CompilerParams(vmem_limit_bytes=24 * 2**20),
    )(*groups, gate_w, up_w, down_w, table)


def table_kernel(chip_ref, ids_hbm, weights_hbm, gain_hbm, *refs):
    near_ref, far_ref, gain_ref, ids_ref, weights_ref, sems = refs[-6:]
    pairs = ((ids_hbm, ids_ref), (weights_hbm, weights_ref), (gain_hbm, gain_ref))
    copies = [pltpu.make_async_copy(a, b, sems.at[i]) for i, (a, b) in enumerate(pairs)]
    for copy in copies:
        copy.start()
    for copy in copies:
        copy.wait()
    chosen, rows = ids_ref.shape
    half = near_ref.shape[1]
    expert = chip_ref[0] ^ lax.broadcasted_iota(jnp.int32, (2 * half, rows), 0)
    table = jnp.zeros((2 * half, rows), jnp.float32)
    for k in range(chosen):
        table += jnp.where(ids_ref[k : k + 1, :] == expert, weights_ref[k : k + 1, :], 0.0)
    near_ref[...] = table[:half].T
    far_ref[...] = table[half:].T


def tables(chip, expert_ids, expert_weights, gain, half, beside):
    rows, chosen = expert_ids.shape
    vmem, hbm = pl.BlockSpec(memory_space=pltpu.VMEM), pl.BlockSpec(memory_space=pltpu.HBM)
    table = jax.ShapeDtypeStruct((rows, half), jnp.float32)
    in_hbm = [
        pltpu.with_memory_space_constraint(a, pltpu.HBM) for a in (expert_ids.T, expert_weights.T, gain, *beside)
    ]
    return pl.pallas_call(
        table_kernel,
        out_shape=(table, table, jax.ShapeDtypeStruct(gain.shape, gain.dtype)),
        in_specs=[pl.BlockSpec(memory_space=pltpu.SMEM)] + [hbm] * len(in_hbm),
        out_specs=(vmem,) * 3,
        scratch_shapes=[
            pltpu.VMEM((chosen, rows), expert_ids.dtype),
            pltpu.VMEM((chosen, rows), expert_weights.dtype),
            pltpu.SemaphoreType.DMA((3,)),
        ],
        cost_estimate=pl.CostEstimate(
            flops=0, bytes_accessed=sum(a.size * a.dtype.itemsize for a in beside), transcendentals=0
        ),
        compiler_params=pltpu.CompilerParams(vmem_limit_bytes=8 * 2**20),
    )(chip, *in_hbm)


def halves(residual, norm_gain, expert_ids, expert_weights, gate_proj, up_proj, down_proj):
    rows, model = residual.shape
    chips = lax.axis_size("expert") // 2
    half = chips // 2

    def across(value, mask):
        pairs = [(i, i ^ (2 * mask)) for i in range(2 * chips)]
        return lax.ppermute(value, "expert", pairs) if mask else value

    def swap(value):
        return partner(value, "expert", 0)

    x = residual
    mirrored = across(x, half)
    near = [across(x, mask) for mask in range(1, half)]
    chip = (lax.axis_index("expert") // 2).reshape(1)
    held = (gate_proj[0].T, up_proj[0].T, down_proj[0])
    near_weights, far_weights, gain = tables(chip, expert_ids, expert_weights, norm_gain, half, held)
    (mirrored,) = pack(([mirrored],), gain, (near_weights,))
    far = [across(mirrored, mask) for mask in range(1, half)]
    mirror_swapped = swap(mirrored)
    far_swapped = [swap(block) for block in far]
    (near_rows,) = pack(([x] + near,), gain, (mirror_swapped, *far))
    *parts, far_weights = expert_parts(
        (mirror_swapped, *far_swapped, mirrored, *far, swap(near_rows), near_rows),
        (half * rows,) * 4,
        *held,
        far_weights,
    )
    mirror_weights = across(far_weights, half)

    def give_back(done):
        done = done.reshape(half, rows, model)
        return [across(done[mask], mask) for mask in range(half)]

    far_blocks = give_back(pair_sum(parts[1], swap(parts[0])))
    near_blocks = give_back(pair_sum(parts[3], swap(parts[2])))
    total = x.astype(jnp.float32) + across(mixed(mirror_weights, far_blocks), half).astype(jnp.float32)
    for mask, block in enumerate(near_blocks):
        total += near_weights[:, mask][:, None] * block.astype(jnp.float32)
    return total.astype(jnp.bfloat16)


def body(residual, norm_gain, expert_ids, expert_weights, gate_proj, up_proj, down_proj):
    rows, chosen = expert_ids.shape
    chips = lax.axis_size("expert") // 2
    whole = 2 * rows * chosen // chips >= rows and chips >= 4 and chips & (chips - 1) == 0
    plan = halves if whole else slots
    return plan(residual, norm_gain, expert_ids, expert_weights, gate_proj, up_proj, down_proj)


def solution(mesh):
    in_specs = (
        P(("groups", "expert"), None),
        P(),
        P(("groups", "expert"), None),
        P(("groups", "expert"), None),
        P("expert", None, None),
        P("expert", None, None),
        P("expert", None, None),
    )
    out_specs = P(("groups", "expert"), None)
    return jax.shard_map(body, mesh=mesh, in_specs=in_specs, out_specs=out_specs, check_vma=False)
```

```python
import functools

import jax
import jax.numpy as jnp
from jax import lax
from jax.experimental import pallas as pl
from jax.experimental.pallas import tpu as pltpu
from jax.sharding import PartitionSpec as P


def partner(value, axis, bit):
    mask = 2**bit
    pairs = [(source, source ^ mask) for source in range(lax.axis_size(axis))]
    return lax.ppermute(value, axis, pairs)


def expert_half(flat, gate_w, up_w, down_w):
    gate = jnp.dot(flat, gate_w, preferred_element_type=jnp.float32)
    upper = jnp.dot(flat, up_w, preferred_element_type=jnp.float32)
    act = (gate * jax.nn.sigmoid(1.702 * gate) * (upper + 1.0)).astype(jnp.bfloat16)
    return jnp.dot(act, down_w, preferred_element_type=jnp.float32).astype(jnp.bfloat16)


def normalised(rows, norm_gain):
    x = rows.astype(jnp.float32)
    scale = lax.rsqrt(jnp.mean(x * x, axis=-1, keepdims=True) + 1e-05)
    return (x * scale * norm_gain).astype(jnp.bfloat16)


def pair_sum(mine, theirs):
    return (mine.astype(jnp.float32) + theirs.astype(jnp.float32)).astype(jnp.bfloat16)


def slots(residual, norm_gain, expert_ids, expert_weights, gate_proj, up_proj, down_proj):
    rows, model = residual.shape
    chosen = expert_ids.shape[1]
    devices = lax.axis_size("expert")
    experts = devices // 2
    capacity = 2 * rows * chosen // experts
    half_cap = capacity // 2
    gate_w, up_w, down_w = (gate_proj[0], up_proj[0], down_proj[0])
    normed = normalised(residual, norm_gain)
    flat_ids = expert_ids.reshape(rows * chosen)
    onehot = (
        flat_ids[:, None] == lax.broadcasted_iota(jnp.int32, (rows * chosen, experts), 1)
    ).astype(jnp.int32)
    slot = jnp.sum(onehot * jnp.cumsum(onehot, axis=0), axis=1) - 1
    position = flat_ids * capacity + slot
    pick = (
        position[:, None] == lax.broadcasted_iota(jnp.int32, (rows * chosen, experts * capacity), 1)
    ).astype(jnp.float32)
    place_rows = jnp.sum(pick.reshape(rows, chosen, experts * capacity), axis=1)
    send = lax.dot_general(
        place_rows.astype(jnp.bfloat16),
        normed,
        (((0,), (0,)), ((), ())),
        preferred_element_type=jnp.float32,
    )
    outgoing = send.astype(jnp.bfloat16).reshape(devices, half_cap, model)
    arrived = lax.all_to_all(outgoing, "expert", split_axis=0, concat_axis=0, tiled=True)
    other = partner(arrived, "expert", 0)
    both = jnp.stack((arrived, other)).reshape(2 * devices * half_cap, model)
    both = expert_half(both, gate_w, up_w, down_w).reshape(2, devices, half_cap, model)
    returned = partner(both[1], "expert", 0)
    finished = pair_sum(both[0], returned)
    back = lax.all_to_all(finished, "expert", split_axis=0, concat_axis=0, tiled=True)
    weighted = jnp.sum(
        (pick * expert_weights.reshape(rows * chosen)[:, None]).reshape(
            rows, chosen, experts * capacity
        ),
        axis=1,
    )
    combined = jnp.dot(
        weighted,
        back.reshape(experts * capacity, model).astype(jnp.float32),
        precision=lax.Precision.HIGHEST,
    )
    return (residual.astype(jnp.float32) + combined).astype(jnp.bfloat16)


def pack_kernel(after, sizes, *refs):
    blocks, gain_ref, outs = refs[after : -1 - len(sizes)], refs[-1 - len(sizes)], refs[-len(sizes) :]
    rows, model = blocks[0].shape
    gain = gain_ref[...].reshape(1, model)
    places = [(out, i) for out, size in zip(outs, sizes) for i in range(size)]
    for block, (out_ref, i) in zip(blocks, places):
        x = block[...].astype(jnp.float32)
        scale = lax.rsqrt(jnp.mean(x * x, axis=-1, keepdims=True) + 1e-05)
        out_ref[pl.ds(i * rows, rows), :] = (x * scale * gain).astype(jnp.bfloat16)


def pack(groups, gain, after):
    blocks = sum(groups, [])
    sizes = tuple(len(group) for group in groups)
    rows, model = blocks[0].shape
    vmem = pl.BlockSpec(memory_space=pltpu.VMEM)
    return pl.pallas_call(
        functools.partial(pack_kernel, len(after), sizes),
        out_shape=tuple(jax.ShapeDtypeStruct((rows * size, model), jnp.bfloat16) for size in sizes),
        in_specs=[pl.BlockSpec(memory_space=pl.ANY)] * len(after) + [vmem] * (len(blocks) + 1),
        out_specs=(vmem,) * len(sizes),
        compiler_params=pltpu.CompilerParams(vmem_limit_bytes=8 * 2**20),
    )(*after, *blocks, gain)


def mix_kernel(table_ref, *refs):
    blocks, out_ref = refs[:-1], refs[-1]
    total = jnp.zeros(out_ref.shape, jnp.float32)
    for i, block in enumerate(blocks):
        total += table_ref[:, i : i + 1] * block[...].astype(jnp.float32)
    out_ref[...] = total.astype(out_ref.dtype)


def mixed(table, blocks):
    vmem = pl.BlockSpec(memory_space=pltpu.VMEM)
    return pl.pallas_call(
        mix_kernel,
        out_shape=jax.ShapeDtypeStruct(blocks[0].shape, blocks[0].dtype),
        in_specs=[vmem] * (len(blocks) + 1),
        out_specs=vmem,
        compiler_params=pltpu.CompilerParams(vmem_limit_bytes=8 * 2**20),
    )(table, *blocks)


def expert_kernel(count, *refs):
    groups, (gate_ref, up_ref, down_ref, table_ref) = refs[:count], refs[count : count + 4]
    outs, table_out_ref = refs[count + 4 : -1], refs[-1]
    table_out_ref[...] = table_ref[...]
    normed = jnp.concatenate([group[...] for group in groups])
    across = (((1,), (1,)), ((), ()))
    gate = lax.dot_general(gate_ref[...], normed, across, preferred_element_type=jnp.float32)
    upper = lax.dot_general(up_ref[...], normed, across, preferred_element_type=jnp.float32)
    act = (gate * jax.nn.sigmoid(1.702 * gate) * (upper + 1.0)).astype(jnp.bfloat16).T
    out = jnp.dot(act, down_ref[...], preferred_element_type=jnp.float32).astype(jnp.bfloat16)
    start = 0
    for out_ref in outs:
        rows = out_ref.shape[0]
        out_ref[...] = out[start : start + rows]
        start += rows


def expert_parts(groups, sizes, gate_w, up_w, down_w, table):
    count, rows = len(groups), sum(sizes)
    hidden, model = gate_w.shape
    vmem = pl.BlockSpec(memory_space=pltpu.VMEM)
    return pl.pallas_call(
        functools.partial(expert_kernel, count),
        out_shape=tuple(jax.ShapeDtypeStruct((size, model), jnp.bfloat16) for size in sizes)
        + (jax.ShapeDtypeStruct(table.shape, table.dtype),),
        in_specs=[vmem] * (count + 4),
        out_specs=(vmem,) * (len(sizes) + 1),
        cost_estimate=pl.CostEstimate(
            flops=6 * rows * model * hidden, bytes_accessed=6 * model * hidden, transcendentals=rows * hidden
        ),
        compiler_params=pltpu.CompilerParams(vmem_limit_bytes=24 * 2**20),
    )(*groups, gate_w, up_w, down_w, table)


def table_kernel(chip_ref, ids_hbm, weights_hbm, gain_hbm, *refs):
    near_ref, far_ref, gain_ref, ids_ref, weights_ref, sems = refs[-6:]
    pairs = ((ids_hbm, ids_ref), (weights_hbm, weights_ref), (gain_hbm, gain_ref))
    copies = [pltpu.make_async_copy(a, b, sems.at[i]) for i, (a, b) in enumerate(pairs)]
    for copy in copies:
        copy.start()
    for copy in copies:
        copy.wait()
    chosen, rows = ids_ref.shape
    half = near_ref.shape[1]
    expert = chip_ref[0] ^ lax.broadcasted_iota(jnp.int32, (2 * half, rows), 0)
    table = jnp.zeros((2 * half, rows), jnp.float32)
    for k in range(chosen):
        table += jnp.where(ids_ref[k : k + 1, :] == expert, weights_ref[k : k + 1, :], 0.0)
    near_ref[...] = table[:half].T
    far_ref[...] = table[half:].T


def tables(chip, expert_ids, expert_weights, gain, half, beside):
    rows, chosen = expert_ids.shape
    vmem, hbm = pl.BlockSpec(memory_space=pltpu.VMEM), pl.BlockSpec(memory_space=pltpu.HBM)
    table = jax.ShapeDtypeStruct((rows, half), jnp.float32)
    in_hbm = [
        pltpu.with_memory_space_constraint(a, pltpu.HBM) for a in (expert_ids.T, expert_weights.T, gain, *beside)
    ]
    return pl.pallas_call(
        table_kernel,
        out_shape=(table, table, jax.ShapeDtypeStruct(gain.shape, gain.dtype)),
        in_specs=[pl.BlockSpec(memory_space=pltpu.SMEM)] + [hbm] * len(in_hbm),
        out_specs=(vmem,) * 3,
        scratch_shapes=[
            pltpu.VMEM((chosen, rows), expert_ids.dtype),
            pltpu.VMEM((chosen, rows), expert_weights.dtype),
            pltpu.SemaphoreType.DMA((3,)),
        ],
        cost_estimate=pl.CostEstimate(
            flops=0, bytes_accessed=sum(a.size * a.dtype.itemsize for a in beside), transcendentals=0
        ),
        compiler_params=pltpu.CompilerParams(vmem_limit_bytes=8 * 2**20),
    )(chip, *in_hbm)


def halves(residual, norm_gain, expert_ids, expert_weights, gate_proj, up_proj, down_proj):
    rows, model = residual.shape
    chips = lax.axis_size("expert") // 2
    half = chips // 2

    def across(value, mask):
        pairs = [(i, i ^ (2 * mask)) for i in range(2 * chips)]
        return lax.ppermute(value, "expert", pairs) if mask else value

    def swap(value):
        return partner(value, "expert", 0)

    x = residual
    mirrored = across(x, half)
    order = [0] + sorted(range(1, half), key=lambda mask: (mask == half // 2, mask % 2 == 0, mask))
    near = [across(x, mask) for mask in order[1:]]
    chip = (lax.axis_index("expert") // 2).reshape(1)
    held = (gate_proj[0].T, up_proj[0].T, down_proj[0])
    near_weights, far_weights, gain = tables(chip, expert_ids, expert_weights, norm_gain, half, held)
    (mirrored,) = pack(([mirrored],), gain, (near_weights,))
    far = [across(mirrored, mask) for mask in range(1, half)]
    mirror_swapped = swap(mirrored)
    far_swapped = [swap(block) for block in far]
    (near_rows,) = pack(([x] + near,), gain, (mirror_swapped, *far))
    *parts, far_weights = expert_parts(
        (mirror_swapped, *far_swapped, mirrored, *far, swap(near_rows), near_rows),
        (half * rows,) * 4,
        *held,
        far_weights,
    )
    mirror_weights = across(far_weights, half)

    def give_back(done, masks):
        done = done.reshape(half, rows, model)
        blocks = [across(done[i], mask) for i, mask in enumerate(masks)]
        return [blocks[masks.index(mask)] for mask in range(half)]

    far_blocks = give_back(pair_sum(parts[1], swap(parts[0])), list(range(half)))
    near_blocks = give_back(pair_sum(parts[3], swap(parts[2])), order)
    total = x.astype(jnp.float32) + across(mixed(mirror_weights, far_blocks), half).astype(jnp.float32)
    for mask, block in enumerate(near_blocks):
        total += near_weights[:, mask][:, None] * block.astype(jnp.float32)
    return total.astype(jnp.bfloat16)


def body(residual, norm_gain, expert_ids, expert_weights, gate_proj, up_proj, down_proj):
    rows, chosen = expert_ids.shape
    chips = lax.axis_size("expert") // 2
    whole = 2 * rows * chosen // chips >= rows and chips >= 4 and chips & (chips - 1) == 0
    plan = halves if whole else slots
    return plan(residual, norm_gain, expert_ids, expert_weights, gate_proj, up_proj, down_proj)


def solution(mesh):
    in_specs = (
        P(("groups", "expert"), None),
        P(),
        P(("groups", "expert"), None),
        P(("groups", "expert"), None),
        P("expert", None, None),
        P("expert", None, None),
        P("expert", None, None),
    )
    out_specs = P(("groups", "expert"), None)
    return jax.shard_map(body, mesh=mesh, in_specs=in_specs, out_specs=out_specs, check_vma=False)
```

```python
import functools

import jax
import jax.numpy as jnp
from jax import lax
from jax.experimental import pallas as pl
from jax.experimental.pallas import tpu as pltpu
from jax.sharding import PartitionSpec as P


def partner(value, axis, bit):
    mask = 2**bit
    pairs = [(source, source ^ mask) for source in range(lax.axis_size(axis))]
    return lax.ppermute(value, axis, pairs)


def expert_half(flat, gate_w, up_w, down_w):
    gate = jnp.dot(flat, gate_w, preferred_element_type=jnp.float32)
    upper = jnp.dot(flat, up_w, preferred_element_type=jnp.float32)
    act = (gate * jax.nn.sigmoid(1.702 * gate) * (upper + 1.0)).astype(jnp.bfloat16)
    return jnp.dot(act, down_w, preferred_element_type=jnp.float32).astype(jnp.bfloat16)


def normalised(rows, norm_gain):
    x = rows.astype(jnp.float32)
    scale = lax.rsqrt(jnp.mean(x * x, axis=-1, keepdims=True) + 1e-05)
    return (x * scale * norm_gain).astype(jnp.bfloat16)


def pair_sum(mine, theirs):
    return (mine.astype(jnp.float32) + theirs.astype(jnp.float32)).astype(jnp.bfloat16)


def slots(residual, norm_gain, expert_ids, expert_weights, gate_proj, up_proj, down_proj):
    rows, model = residual.shape
    chosen = expert_ids.shape[1]
    devices = lax.axis_size("expert")
    experts = devices // 2
    capacity = 2 * rows * chosen // experts
    half_cap = capacity // 2
    gate_w, up_w, down_w = (gate_proj[0], up_proj[0], down_proj[0])
    normed = normalised(residual, norm_gain)
    flat_ids = expert_ids.reshape(rows * chosen)
    onehot = (
        flat_ids[:, None] == lax.broadcasted_iota(jnp.int32, (rows * chosen, experts), 1)
    ).astype(jnp.int32)
    slot = jnp.sum(onehot * jnp.cumsum(onehot, axis=0), axis=1) - 1
    position = flat_ids * capacity + slot
    pick = (
        position[:, None] == lax.broadcasted_iota(jnp.int32, (rows * chosen, experts * capacity), 1)
    ).astype(jnp.float32)
    place_rows = jnp.sum(pick.reshape(rows, chosen, experts * capacity), axis=1)
    send = lax.dot_general(
        place_rows.astype(jnp.bfloat16),
        normed,
        (((0,), (0,)), ((), ())),
        preferred_element_type=jnp.float32,
    )
    outgoing = send.astype(jnp.bfloat16).reshape(devices, half_cap, model)
    arrived = lax.all_to_all(outgoing, "expert", split_axis=0, concat_axis=0, tiled=True)
    other = partner(arrived, "expert", 0)
    both = jnp.stack((arrived, other)).reshape(2 * devices * half_cap, model)
    both = expert_half(both, gate_w, up_w, down_w).reshape(2, devices, half_cap, model)
    returned = partner(both[1], "expert", 0)
    finished = pair_sum(both[0], returned)
    back = lax.all_to_all(finished, "expert", split_axis=0, concat_axis=0, tiled=True)
    weighted = jnp.sum(
        (pick * expert_weights.reshape(rows * chosen)[:, None]).reshape(
            rows, chosen, experts * capacity
        ),
        axis=1,
    )
    combined = jnp.dot(
        weighted,
        back.reshape(experts * capacity, model).astype(jnp.float32),
        precision=lax.Precision.HIGHEST,
    )
    return (residual.astype(jnp.float32) + combined).astype(jnp.bfloat16)


def pack_kernel(after, sizes, *refs):
    blocks, gain_ref, outs = refs[after : -1 - len(sizes)], refs[-1 - len(sizes)], refs[-len(sizes) :]
    rows, model = blocks[0].shape
    gain = gain_ref[...].reshape(1, model)
    places = [(out, i) for out, size in zip(outs, sizes) for i in range(size)]
    for block, (out_ref, i) in zip(blocks, places):
        x = block[...].astype(jnp.float32)
        scale = lax.rsqrt(jnp.mean(x * x, axis=-1, keepdims=True) + 1e-05)
        out_ref[pl.ds(i * rows, rows), :] = (x * scale * gain).astype(jnp.bfloat16)


def pack(groups, gain, after):
    blocks = sum(groups, [])
    sizes = tuple(len(group) for group in groups)
    rows, model = blocks[0].shape
    vmem = pl.BlockSpec(memory_space=pltpu.VMEM)
    return pl.pallas_call(
        functools.partial(pack_kernel, len(after), sizes),
        out_shape=tuple(jax.ShapeDtypeStruct((rows * size, model), jnp.bfloat16) for size in sizes),
        in_specs=[pl.BlockSpec(memory_space=pl.ANY)] * len(after) + [vmem] * (len(blocks) + 1),
        out_specs=(vmem,) * len(sizes),
        compiler_params=pltpu.CompilerParams(vmem_limit_bytes=8 * 2**20),
    )(*after, *blocks, gain)


def mix_kernel(table_ref, *refs):
    blocks, out_ref = refs[:-1], refs[-1]
    total = jnp.zeros(out_ref.shape, jnp.float32)
    for i, block in enumerate(blocks):
        total += table_ref[:, i : i + 1] * block[...].astype(jnp.float32)
    out_ref[...] = total.astype(out_ref.dtype)


def mixed(table, blocks):
    vmem = pl.BlockSpec(memory_space=pltpu.VMEM)
    return pl.pallas_call(
        mix_kernel,
        out_shape=jax.ShapeDtypeStruct(blocks[0].shape, blocks[0].dtype),
        in_specs=[vmem] * (len(blocks) + 1),
        out_specs=vmem,
        compiler_params=pltpu.CompilerParams(vmem_limit_bytes=8 * 2**20),
    )(table, *blocks)


def expert_kernel(count, *refs):
    groups, (gate_ref, up_ref, down_ref, table_ref) = refs[:count], refs[count : count + 4]
    outs, table_out_ref = refs[count + 4 : -1], refs[-1]
    table_out_ref[...] = table_ref[...]
    normed = jnp.concatenate([group[...] for group in groups])
    across = (((1,), (1,)), ((), ()))
    gate = lax.dot_general(gate_ref[...], normed, across, preferred_element_type=jnp.float32)
    upper = lax.dot_general(up_ref[...], normed, across, preferred_element_type=jnp.float32)
    act = (gate * (0.5 * jnp.tanh(0.851 * gate) + 0.5) * (upper + 1.0)).astype(jnp.bfloat16).T
    out = jnp.dot(act, down_ref[...], preferred_element_type=jnp.float32).astype(jnp.bfloat16)
    start = 0
    for out_ref in outs:
        rows = out_ref.shape[0]
        out_ref[...] = out[start : start + rows]
        start += rows


def expert_parts(groups, sizes, gate_w, up_w, down_w, table):
    count, rows = len(groups), sum(sizes)
    hidden, model = gate_w.shape
    vmem = pl.BlockSpec(memory_space=pltpu.VMEM)
    return pl.pallas_call(
        functools.partial(expert_kernel, count),
        out_shape=tuple(jax.ShapeDtypeStruct((size, model), jnp.bfloat16) for size in sizes)
        + (jax.ShapeDtypeStruct(table.shape, table.dtype),),
        in_specs=[vmem] * (count + 4),
        out_specs=(vmem,) * (len(sizes) + 1),
        cost_estimate=pl.CostEstimate(
            flops=6 * rows * model * hidden, bytes_accessed=6 * model * hidden, transcendentals=rows * hidden
        ),
        compiler_params=pltpu.CompilerParams(vmem_limit_bytes=24 * 2**20),
    )(*groups, gate_w, up_w, down_w, table)


def table_kernel(chip_ref, ids_hbm, weights_hbm, gain_hbm, *refs):
    near_ref, far_ref, gain_ref, ids_ref, weights_ref, sems = refs[-6:]
    pairs = ((ids_hbm, ids_ref), (weights_hbm, weights_ref), (gain_hbm, gain_ref))
    copies = [pltpu.make_async_copy(a, b, sems.at[i]) for i, (a, b) in enumerate(pairs)]
    for copy in copies:
        copy.start()
    for copy in copies:
        copy.wait()
    chosen, rows = ids_ref.shape
    half = near_ref.shape[1]
    expert = chip_ref[0] ^ lax.broadcasted_iota(jnp.int32, (2 * half, rows), 0)
    table = jnp.zeros((2 * half, rows), jnp.float32)
    for k in range(chosen):
        table += jnp.where(ids_ref[k : k + 1, :] == expert, weights_ref[k : k + 1, :], 0.0)
    near_ref[...] = table[:half].T
    far_ref[...] = table[half:].T


def tables(chip, expert_ids, expert_weights, gain, half, beside):
    rows, chosen = expert_ids.shape
    vmem, hbm = pl.BlockSpec(memory_space=pltpu.VMEM), pl.BlockSpec(memory_space=pltpu.HBM)
    table = jax.ShapeDtypeStruct((rows, half), jnp.float32)
    in_hbm = [
        pltpu.with_memory_space_constraint(a, pltpu.HBM) for a in (expert_ids.T, expert_weights.T, gain, *beside)
    ]
    return pl.pallas_call(
        table_kernel,
        out_shape=(table, table, jax.ShapeDtypeStruct(gain.shape, gain.dtype)),
        in_specs=[pl.BlockSpec(memory_space=pltpu.SMEM)] + [hbm] * len(in_hbm),
        out_specs=(vmem,) * 3,
        scratch_shapes=[
            pltpu.VMEM((chosen, rows), expert_ids.dtype),
            pltpu.VMEM((chosen, rows), expert_weights.dtype),
            pltpu.SemaphoreType.DMA((3,)),
        ],
        cost_estimate=pl.CostEstimate(
            flops=0, bytes_accessed=sum(a.size * a.dtype.itemsize for a in beside), transcendentals=0
        ),
        compiler_params=pltpu.CompilerParams(vmem_limit_bytes=8 * 2**20),
    )(chip, *in_hbm)


def halves(residual, norm_gain, expert_ids, expert_weights, gate_proj, up_proj, down_proj):
    rows, model = residual.shape
    chips = lax.axis_size("expert") // 2
    half = chips // 2

    def across(value, mask):
        pairs = [(i, i ^ (2 * mask)) for i in range(2 * chips)]
        return lax.ppermute(value, "expert", pairs) if mask else value

    def swap(value):
        return partner(value, "expert", 0)

    x = residual
    mirrored = across(x, half)
    near = [across(x, mask) for mask in range(1, half)]
    chip = (lax.axis_index("expert") // 2).reshape(1)
    held = (gate_proj[0].T, up_proj[0].T, down_proj[0])
    near_weights, far_weights, gain = tables(chip, expert_ids, expert_weights, norm_gain, half, held)
    (mirrored,) = pack(([mirrored],), gain, (near_weights,))
    far = [across(mirrored, mask) for mask in range(1, half)]
    mirror_swapped = swap(mirrored)
    far_swapped = [swap(block) for block in far]
    (near_rows,) = pack(([x] + near,), gain, (mirror_swapped, *far))
    *parts, far_weights = expert_parts(
        (mirror_swapped, *far_swapped, mirrored, *far, swap(near_rows), near_rows),
        (half * rows,) * 4,
        *held,
        far_weights,
    )
    mirror_weights = across(far_weights, half)

    def give_back(done):
        done = done.reshape(half, rows, model)
        return [across(done[mask], mask) for mask in range(half)]

    far_blocks = give_back(pair_sum(parts[1], swap(parts[0])))
    near_blocks = give_back(pair_sum(parts[3], swap(parts[2])))
    total = x.astype(jnp.float32) + across(mixed(mirror_weights, far_blocks), half).astype(jnp.float32)
    for mask, block in enumerate(near_blocks):
        total += near_weights[:, mask][:, None] * block.astype(jnp.float32)
    return total.astype(jnp.bfloat16)


def body(residual, norm_gain, expert_ids, expert_weights, gate_proj, up_proj, down_proj):
    rows, chosen = expert_ids.shape
    chips = lax.axis_size("expert") // 2
    whole = 2 * rows * chosen // chips >= rows and chips >= 4 and chips & (chips - 1) == 0
    plan = halves if whole else slots
    return plan(residual, norm_gain, expert_ids, expert_weights, gate_proj, up_proj, down_proj)


def solution(mesh):
    in_specs = (
        P(("groups", "expert"), None),
        P(),
        P(("groups", "expert"), None),
        P(("groups", "expert"), None),
        P("expert", None, None),
        P("expert", None, None),
        P("expert", None, None),
    )
    out_specs = P(("groups", "expert"), None)
    return jax.shard_map(body, mesh=mesh, in_specs=in_specs, out_specs=out_specs, check_vma=False)
```
